256 devices in a mesh: maprow: 16 (over x, y), mapcol: 8 (over z), sect: 2 (over core).
Axes of the slice: x: 4, y: 4, z: 8, core: 2. Of those that a mesh axis runs over, the one named last changes fastest.
Arguments:
- elevation: float32 [4096, 8192], P('maprow', ('mapcol', 'sect')), may hold values from -60 to 60
- layover: int32 [4096, 8192], P('maprow', ('mapcol', 'sect')), may hold values 0 or 1
- footprint_pixel: int32 [4096, 8192], P('maprow', ('mapcol', 'sect')), may hold values from 0 to 127
- footprint_device: int32 [256, 512, 1], P(('maprow', 'mapcol', 'sect')), may hold values from 0 to 127; in each aligned block of 512 rows (0 to 511, 512 to 1023, ..., all dimensions but the last counted through in order) at most 8 rows name the same one
- local_block: int32 [256, 512], P(('maprow', 'mapcol', 'sect')), may hold values from 0 to 127
- backscatter: float32 [32768, 128], P(('maprow', 'mapcol', 'sect')), may hold values from 0.5 to 8
Outputs:
- gamma_radar: float32 [32768, 128], P(('maprow', 'mapcol', 'sect'))
- gamma_map: float32 [4096, 8192], P('maprow', ('mapcol', 'sect'))
The draws below stay inside these ranges and needn't reach their ends.
Inputs may be any that keep to these rules, and one draw needn't show every extreme that they name: `footprint_device`: among the 512 footprint blocks of one tile at most 8 name the same radar device; some tile reaches 8.
All inputs are finite; a program needn't handle non-finite values. No bound on the sum of `layover` on one device may be relied on, other than what follows from the above.
Results may differ from the reference program's by a relative error of at most 0.000068.
Values sent between devices are 32-bit elements; how exact they have to be, the bound alone decides.
A program may use at most 64 MiB of HBM per device.

```python
import math
import jax
import jax.numpy as jnp
import numpy as np

TR = 256
TC = 512
BR = 16
BC = 16
PIX = 128
TB = 512
RB_DEV = 128
CAP = 8
MR = 4096
MC = 8192
NRB = 32768
N_MAPROW = 16
N_MAPCOL = 8
N_SECT = 2


def place_ends(array, key, low, largest):
    longest = array.shape.index(max(array.shape))
    spots = []
    for shift in (0, 1):
        where = [jax.random.randint(jax.random.fold_in(key, axis), (), 0, length) for axis, length in enumerate(array.shape)]
        where[longest] = (where[longest] + shift) % array.shape[longest]
        spots.append(tuple(where))
    return array.at[spots[0]].set(low).at[spots[1]].set(largest)


def shard_levels(own_key, extent, pieces, low, high):
    loudness, own = 1.0, jax.random.fold_in(own_key, 6)
    for axis_at, blocks in pieces:
        steps = jnp.exp(jax.random.uniform(jax.random.fold_in(own, axis_at), (blocks,), jnp.float32, low / len(pieces), high / len(pieces)))
        loudness = loudness * jnp.repeat(steps, extent[axis_at] // blocks).reshape([-1 if axis == axis_at else 1 for axis in range(len(extent))])
    return loudness


def routed_block(rng, own, number, rows, count, top, bound, lean):
    ranking = jax.random.permutation(rng, count)
    crowded, ordinary = shares(count, rows * top, bound, lean, True), shares(count, rows * top, bound, lean, False)
    places = jnp.arange(count)

    def named(tallies, rotation):
        used = int((tallies > 0).sum())
        fixed = max(1, used // 4)
        moved = fixed + (places - fixed + rotation * (used - fixed)) % max(1, count - fixed)
        return jnp.zeros((count,), jnp.int32).at[ranking[jnp.where(places < fixed, places, moved)]].set(jnp.asarray(tallies, jnp.int32))

    tallies = jnp.where(number % 4 == 0, named(crowded, number // 4), named(ordinary, number - number // 4 - 1))
    mixed = jax.random.permutation(jax.random.fold_in(own, 3), count)
    giver, taker = mixed[0:count // 2 * 2:2], mixed[1:count // 2 * 2:2]
    slack = jnp.minimum(tallies[giver] - 1, bound - tallies[taker]) // 2
    slack = jnp.where((giver == ranking[0]) | (taker == ranking[0]) | (tallies[taker] == 0), 0, jnp.maximum(slack, 0))
    moved = jax.random.randint(jax.random.fold_in(own, 4), (count // 2,), 0, 1 << 20) % (slack + 1)
    tallies = tallies.at[giver].add(-moved).at[taker].add(moved)
    labels = jnp.searchsorted(jnp.cumsum(tallies), jnp.arange(rows * top), side="right").astype(jnp.int32)
    listing = labels.reshape(top, rows).T
    listing = listing[jax.random.permutation(jax.random.fold_in(own, 1), rows)]
    rotation = jax.random.randint(jax.random.fold_in(own, 2), (rows, 1), 0, top)
    return jnp.take_along_axis(listing, (jnp.arange(top)[None, :] + rotation) % top, axis=1)


def shares(count, total, most, lean, full):
    portions = [(1 << 20) // math.isqrt(standing ** lean) + 1 for standing in range(1, count + 1)]
    largest = most if full else min(most, max(-(-total // count), total * portions[0] // sum(portions)))
    least = 1 if total - largest >= count - 1 else 0
    counts, rest = [largest] + [least] * (count - 1), total - largest - least * (count - 1)
    while rest > 0:
        free = [i for i in range(1, count) if counts[i] < largest] or [i for i in range(1, count) if counts[i] < most]
        pool, budget = sum([portions[i] for i in free]), rest
        for i in free:
            more = min(most - counts[i], max(1, budget * portions[i] // pool), rest)
            counts[i] = counts[i] + more
            rest = rest - more
    return np.array(counts)


def normal_values(key, dims, deviation, reach, shards=(), kind=jnp.bfloat16):
    gain = shard_levels(key, dims, shards, -0.22, 0.18) if shards else 1.0
    array = jax.random.normal(key, dims, jnp.float32) * deviation * gain
    return jnp.minimum(jnp.maximum(array, -reach), reach).astype(kind)


def setup_inputs(seed: int = 0) -> dict:
    keys = jax.random.split(jax.random.key(seed), 7)
    elevation = normal_values(keys[0], (MR, MC), 10.0, 60.0, ((0, 16), (1, 16)), jnp.float32)
    layover = place_ends((jax.random.randint(keys[1], (MR, MC), 0, 6) < 1).astype(jnp.int32), jax.random.fold_in(keys[1], 1), 0, 1)
    footprint_pixel = place_ends(jax.random.randint(keys[2], (MR, MC), 0, PIX), jax.random.fold_in(keys[2], 1), 0, PIX - 1).astype(jnp.int32)
    footprint_device_keys = jax.random.split(jax.random.fold_in(keys[3], 1), (N_MAPROW * N_MAPCOL * N_SECT) * TB // TB)
    footprint_device_turns = jax.random.permutation(jax.random.fold_in(keys[3], 3), (N_MAPROW * N_MAPCOL * N_SECT) * TB // TB)
    footprint_device = jax.vmap(lambda own, number: routed_block(jax.random.fold_in(keys[3], 2), own, number, TB, N_MAPROW * N_MAPCOL, 1, CAP, 2))(footprint_device_keys, footprint_device_turns).reshape((N_MAPROW * N_MAPCOL * N_SECT, TB, 1))
    local_block = place_ends(jax.random.randint(keys[4], (N_MAPROW * N_MAPCOL * N_SECT, TB), 0, RB_DEV), jax.random.fold_in(keys[4], 1), 0, RB_DEV - 1).astype(jnp.int32)
    backscatter = jnp.clip(jnp.exp(math.log(8.0) - 2.7725887 * jax.random.uniform(keys[5], (NRB, PIX), jnp.float32) ** shard_levels(keys[5], (NRB, PIX), ((0, 256),), -0.2, 0.2)), 0.5, 8.0)
    return dict(elevation=elevation, layover=layover, footprint_pixel=footprint_pixel, footprint_device=footprint_device, local_block=local_block, backscatter=backscatter)


cell_spacing = 10.0
heading_angle = 0.2


def reference(elevation, layover, footprint_pixel, footprint_device, local_block, backscatter):
    padded = jnp.pad(elevation, 1)
    slope_cols = (padded[1:-1, 2:] - padded[1:-1, :-2]) / (2.0 * cell_spacing)
    slope_rows = (padded[2:, 1:-1] - padded[:-2, 1:-1]) / (2.0 * cell_spacing)
    column = (jnp.arange(MC).astype(jnp.float32) + 0.5) / MC
    incidence = 0.52 + 0.28 * column
    look_cols = -jnp.sin(incidence) * jnp.cos(heading_angle)
    look_rows = -jnp.sin(incidence) * jnp.sin(heading_angle)
    look_up = jnp.cos(incidence)
    facing = -slope_cols * look_cols[None, :] - slope_rows * look_rows[None, :] + look_up[None, :]
    areas = jnp.maximum(facing, 0.0) * (1 - layover).astype(jnp.float32)
    tile_cols = N_MAPCOL * N_SECT
    shape_blocks = (N_MAPROW, tile_cols, TR // BR, TC // BC)
    target = footprint_device[:, :, 0].reshape(shape_blocks)
    within = local_block.reshape(shape_blocks)
    section = (jnp.arange(tile_cols) % N_SECT).astype(jnp.int32)[None, :, None, None]
    block_ids = ((target * N_SECT + section) * RB_DEV + within).astype(jnp.int32)
    block_ids = block_ids.transpose(0, 2, 1, 3)[:, :, None, :, :, None]
    block_ids = jnp.broadcast_to(block_ids, (N_MAPROW, TR // BR, BR, tile_cols, TC // BC, BC)).reshape(MR, MC)
    index_all = block_ids * PIX + footprint_pixel
    area_sum = jax.ops.segment_sum(areas.ravel(), index_all.ravel(), num_segments=NRB * PIX)
    gamma_radar = backscatter / jnp.maximum(area_sum.reshape(NRB, PIX), 1.0)
    gamma_map = gamma_radar.ravel()[index_all]
    return gamma_radar, gamma_map
```

```python
import functools

import jax
import jax.numpy as jnp
from jax import lax
from jax.experimental import pallas as pl
from jax.experimental.pallas import tpu as pltpu
from jax.sharding import PartitionSpec as P

BR = 16
BC = 16
PIX = 128
CELL_SPACING = 10.0
HEADING = 0.2
MESH = pl.DeviceIdType.MESH
F32 = jnp.float32
BF16 = jnp.bfloat16


def iota(shape, dim):
    return lax.broadcasted_iota(jnp.int32, shape, dim)


def iotaf(shape, dim):
    return iota(shape, dim).astype(F32)


def swap_groups(x):
    lane, row = iota((8, 128), 1), iota((8, 128), 0)
    x = pltpu.roll(x, 0, 1, stride=16, stride_axis=0)
    x = jnp.take_along_axis(x, ((lane >> 4) - row) & 7, axis=0)
    return jnp.take_along_axis(x, (lane + 16 * row) & 127, axis=1)


def split(x):
    first = x.astype(BF16)
    return jnp.concatenate([first, (x - first.astype(F32)).astype(BF16)], axis=1)


def folded(x):
    half = x.shape[1] // 2
    return x[:, :half] + x[:, half:]


def dot(a, b):
    return lax.dot_general(a, b, (((1,), (0,)), ((), ())), preferred_element_type=F32)


def dot_nt(a, b):
    return lax.dot_general(a, b, (((1,), (1,)), ((), ())), preferred_element_type=F32)


def block_sums(area, pixel):
    firsts, seconds, lows = [], [], []
    for half in range(2):
        a = swap_groups(area[8 * half : 8 * half + 8])
        p = swap_groups(pixel[8 * half : 8 * half + 8])
        a1 = a.astype(BF16).astype(F32)
        a2 = a - a1
        is_high = (p >> 4)[:, None, :] == iota((8, 8, 128), 1)
        is_low = (p & 15)[:, None, :] == iota((8, 16, 128), 1)
        firsts.append(jnp.where(is_high, a1[:, None, :], 0.0).reshape(64, 128))
        seconds.append(jnp.where(is_high, a2[:, None, :], 0.0).reshape(64, 128))
        lows.append(jnp.where(is_low, 1.0, 0.0).reshape(128, 128))
    left = jnp.concatenate(
        [jnp.concatenate(firsts, axis=1), jnp.concatenate(seconds, axis=1)], axis=0
    ).astype(BF16)
    right = jnp.concatenate(lows, axis=1).astype(BF16)
    out = dot_nt(left, right)
    out = out[:64] + out[64:]
    group = iota((8, 128), 1) >> 4
    own = out[0:8]
    for b in range(1, 8):
        own = jnp.where(group == b, out[8 * b : 8 * b + 8], own)
    return swap_groups(own)


def exchange(
    nr, nz, cap,
    elev, lay, pix, target, local, back,
    gamma, found,
    epad, layv, pixv, look, pmat, pmt, oht, oh, hist, sendb, recvb, idsend, idrecv,
    dense, cin, gin, backb, retb,
    in_sem, halo_send, halo_recv, id_send, id_recv, out_send, out_recv,
    chain_send, chain_recv, gchain_send, gchain_recv, ret_send, ret_recv,
):
    rows, cols = elev.shape
    tb = target.shape[1]
    dests = nr * nz
    h = nz // 2
    tiles = cols // 128
    r, c, s = lax.axis_index("maprow"), lax.axis_index("mapcol"), lax.axis_index("sect")
    up_z, down_z = {"mapcol": lax.rem(c + 1, nz)}, {"mapcol": lax.rem(c + nz - 1, nz)}
    west = {"mapcol": lax.rem(c + nz - 1 + s, nz), "sect": 1 - s}
    east = {"mapcol": lax.rem(c + s, nz), "sect": 1 - s}
    north, south = {"maprow": lax.rem(r + nr - 1, nr)}, {"maprow": lax.rem(r + 1, nr)}
    spans = [(0, 1)] + [(2 * g - 1, 2 * g + 1) for g in range(1, h)] + [(nz - 1, nz)]

    def place(k):
        return 2 * (k - h) if k >= h else 2 * (h - k) - 1

    barrier = pltpu.get_barrier_semaphore()

    def greet(j, carry):
        pl.semaphore_signal(
            barrier, inc=1, device_id={"maprow": lax.rem(r + j, nr)}, device_id_type=MESH
        )
        return carry

    lax.fori_loop(1, nr, greet, 0)
    for neighbour in (up_z, down_z, west, east):
        pl.semaphore_signal(barrier, inc=1, device_id=neighbour, device_id_type=MESH)

    loads = [
        pltpu.make_async_copy(elev, epad.at[8 : 8 + rows, 128 : 128 + cols], in_sem.at[0]),
        pltpu.make_async_copy(lay, layv, in_sem.at[1]),
        pltpu.make_async_copy(pix, pixv, in_sem.at[2]),
    ]
    for load in loads:
        load.start()

    name = target[...]
    step_z = ((name & (nz - 1)) + (nz - c)) & (nz - 1)
    ahead = step_z - h
    order = jnp.where(ahead >= 0, 2 * ahead, -2 * ahead - 1)
    spot = (name >> (nz.bit_length() - 1)) * nz + order
    onehot = iota((dests, tb), 0) == spot
    earlier = jnp.where(iota((tb, tb), 0) < iota((tb, tb), 1), 1.0, 0.0).astype(BF16)
    running = dot(jnp.where(onehot, 1.0, 0.0).astype(BF16), earlier)
    rank = jnp.sum(jnp.where(onehot, running, 0.0), axis=0, keepdims=True)
    slot = (spot * cap).astype(F32) + rank
    ids = jnp.where(onehot, local[...].astype(F32), 0.0).astype(BF16)
    at_lane = (r * cap).astype(F32) + rank
    lanes = jnp.where(iotaf((128, tb), 0) == at_lane, 1.0, 0.0).astype(BF16)
    idsend[...] = dot_nt(ids, lanes).reshape(nr, nz, 128)
    idrecv[pl.ds(r, 1)] = idsend[pl.ds(r, 1)]

    pl.semaphore_wait(barrier, nr - 1 + 4)

    halos = [
        (elev.at[rows - 8 : rows, :], epad.at[0:8, 128 : 128 + cols], south),
        (elev.at[0:8, :], epad.at[rows + 8 : rows + 16, 128 : 128 + cols], north),
        (elev.at[:, cols - 128 : cols], epad.at[8 : 8 + rows, 0:128], east),
        (elev.at[:, 0:128], epad.at[8 : 8 + rows, 128 + cols : 256 + cols], west),
    ]
    halos = [
        pltpu.make_async_remote_copy(
            src_ref=src, dst_ref=dst, send_sem=halo_send.at[i], recv_sem=halo_recv.at[i],
            device_id=where, device_id_type=MESH,
        )
        for i, (src, dst, where) in enumerate(halos)
    ]
    for halo in halos:
        halo.start()

    def to_plane(source, sink, send_sem, recv_sem):
        def body(j, carry):
            peer = lax.rem(r + j, nr)
            pltpu.make_async_remote_copy(
                src_ref=source(peer), dst_ref=sink(r), send_sem=send_sem, recv_sem=recv_sem,
                device_id={"maprow": peer}, device_id_type=MESH,
            ).start()
            return carry

        lax.fori_loop(1, nr, body, 0)

    def arrived(part, sem):
        pltpu.make_async_copy(part, part, sem).wait()

    to_plane(lambda i: idsend.at[i], lambda i: idrecv.at[i], id_send.at[0], id_recv.at[0])

    i0 = iota((128, 1), 0)
    row_slot = ((i0 // cap) * (nz * cap) + lax.rem(i0, cap)).astype(F32)
    i1 = iota((1, 128), 1)
    lane_slot = ((i1 // cap) * (nz * cap) + lax.rem(i1, cap)).astype(F32)
    slot_down = jnp.transpose(jnp.broadcast_to(slot, (128, tb)))
    for p in range(nz):
        pmat[p] = jnp.where(row_slot + float(p * cap) == slot, 1.0, 0.0).astype(BF16)
        pmt[:, 128 * p : 128 * p + 128] = jnp.where(
            slot_down == lane_slot + float(p * cap), 1.0, 0.0
        ).astype(BF16)

    column = ((c * 2 + s) * cols + iota((1, cols), 1)).astype(F32)
    incidence = 0.52 + 0.28 * (column + 0.5) / float(cols * nz * 2)
    sine, heading = jnp.sin(incidence), jnp.full((1, cols), HEADING, F32)
    look[0:1, :] = -sine * jnp.cos(heading) / (2.0 * CELL_SPACING)
    look[1:2, :] = -sine * jnp.sin(heading) / (2.0 * CELL_SPACING)
    look[2:3, :] = jnp.cos(incidence)

    for load in loads:
        load.wait()
    for halo in halos:
        halo.wait_recv()

    @pl.when(r == 0)
    def _():
        epad[0:8, 128 : 128 + cols] = jnp.zeros((8, cols), F32)

    @pl.when(r == nr - 1)
    def _():
        epad[rows + 8 : rows + 16, 128 : 128 + cols] = jnp.zeros((8, cols), F32)

    @pl.when((c == 0) & (s == 0))
    def _():
        epad[8 : 8 + rows, 0:128] = jnp.zeros((rows, 128), F32)

    @pl.when((c == nz - 1) & (s == 1))
    def _():
        epad[8 : 8 + rows, 128 + cols : 256 + cols] = jnp.zeros((rows, 128), F32)

    def band(i, carry):
        top = pl.multiple_of(i * BR, BR)
        lane = iota((BR, 128), 1)
        around = epad[pl.ds(top, 32), 128 : 128 + cols]
        mid = epad[pl.ds(pl.multiple_of(top + 8, 8), BR), :]
        mids = [mid[:, 128 * j : 128 * j + 128] for j in range(tiles + 2)]
        right = [pltpu.roll(x, 1, 1) for x in mids[:-1]]
        left = [pltpu.roll(x, 127, 1) for x in mids[1:]]
        for j in range(tiles):
            at = slice(128 * j, 128 * j + 128)
            before = jnp.where(lane == 0, right[j], right[j + 1])
            after = jnp.where(lane == 127, left[j + 1], left[j])
            rise_cols = after - before
            rise_rows = around[9:25, at] - around[7:23, at]
            facing = (
                look[2:3, at] - rise_cols * look[0:1, at] - rise_rows * look[1:2, at]
            )
            lit = (1 - layv[pl.ds(top, BR), at]).astype(F32)
            area = jnp.maximum(facing, 0.0) * lit
            sums = block_sums(area, pixv[pl.ds(top, BR), at])
            hist[pl.ds(pl.multiple_of(i * (tiles * 8) + 8 * j, 8), 8), :] = sums
        return carry

    lax.fori_loop(0, rows // BR, band, 0)

    terms = split(hist[...])
    for g, (p0, p1) in enumerate(spans):
        for p in range(p0, p1):
            sendb[:, p] = folded(dot(pmat[p], terms)).reshape(nr, cap, PIX)
        recvb[pl.ds(r, 1), p0:p1] = sendb[pl.ds(r, 1), p0:p1]
        to_plane(
            lambda i: sendb.at[i, p0:p1], lambda i: recvb.at[i, p0:p1],
            out_send.at[g], out_recv.at[g],
        )

    arrived(idrecv.at[0 : nr - 1], id_recv.at[0])
    names = idrecv[0]
    for i in range(1, nr):
        names = names + idrecv[i]
    for p in range(nz):
        wide = jnp.broadcast_to(names[p : p + 1, :], (128, 128))
        oht[p] = jnp.where(wide == iotaf((128, 128), 0), 1.0, 0.0).astype(BF16)
        oh[p] = jnp.where(jnp.transpose(wide) == iotaf((128, 128), 1), 1.0, 0.0).astype(BF16)

    def hop(source, sinks, sends, recvs, way, j, q):
        return pltpu.make_async_remote_copy(
            src_ref=source, dst_ref=sinks.at[way, j, q],
            send_sem=sends.at[way, j, q], recv_sem=recvs.at[way, j, q],
            device_id=(up_z, down_z)[way], device_id_type=MESH,
        )

    def pieces(j, last):
        if j == last:
            return [(0, 0), (1, 1)]
        return [(w, q) for q in range(2) for w in range(2)]

    hops = {}
    for g, (p0, p1) in enumerate(spans):
        arrived(recvb.at[0 : nr - 1, p0:p1], out_recv.at[g])
        for p in range(p0, p1):
            dense[p] = folded(dot(oht[p], split(recvb[:, p].reshape(128, PIX))))
        if g < h:
            for way, q in pieces(g + 1, 1):
                p = place(h - g if way == 0 else h + g)
                part = slice(64 * q, 64 * q + 64)
                if (way, g, q) in hops:
                    hops[way, g, q].wait_recv()
                    dense[p, part] = dense[p, part] + cin[way, g, q]
                hops[way, g + 1, q] = hop(
                    dense.at[p, part], cin, chain_send, chain_recv, way, g + 1, q
                )
                hops[way, g + 1, q].start()
        else:
            for q in range(2):
                part = slice(64 * q, 64 * q + 64)
                total = dense[p0, part]
                for way in range(2):
                    if (way, g, q) in hops:
                        hops[way, g, q].wait_recv()
                        total = total + cin[way, g, q]
                gamma[part] = back[part] / jnp.maximum(total, 1.0)

    ghops = {}

    def pass_on(j):
        for way, q in pieces(j, h):
            source = gamma.at[64 * q : 64 * q + 64] if j == 1 else gin.at[way, j - 1, q]
            if j > 1:
                ghops[way, j - 1, q].wait_recv()
            ghops[way, j, q] = hop(source, gin, gchain_send, gchain_recv, way, j, q)
            ghops[way, j, q].start()

    def give(g, tables):
        p0, p1 = spans[g]
        for p, table in zip(range(p0, p1), tables):
            backb[:, p] = folded(dot(oh[p], split(table))).reshape(nr, cap, PIX)
        retb[pl.ds(r, 1), p0:p1] = backb[pl.ds(r, 1), p0:p1]
        to_plane(
            lambda i: backb.at[i, p0:p1], lambda i: retb.at[i, p0:p1],
            ret_send.at[g], ret_recv.at[g],
        )

    def take(g):
        p0, p1 = spans[g]
        arrived(retb.at[0 : nr - 1, p0:p1], ret_recv.at[g])
        given = jnp.concatenate(
            [split(retb[:, p].reshape(128, PIX)) for p in range(p0, p1)], axis=0
        )
        rows_found = folded(dot(pmt[:, 128 * p0 : 128 * p1], given))
        found[...] = rows_found if g == h else found[...] + rows_found

    pass_on(1)
    give(h, [gamma[...]])
    for j in range(1, h):
        pass_on(j + 1)
        for way, q in pieces(j, h):
            if (way, j + 1, q) not in ghops:
                ghops[way, j, q].wait_recv()
        give(h - j, [gin[1, j].reshape(128, PIX), gin[0, j].reshape(128, PIX)])
        take(h - j + 1)
    for way, q in pieces(h, h):
        ghops[way, h, q].wait_recv()
    give(0, [jnp.concatenate([gin[0, h, 0], gin[1, h, 1]], axis=0)])
    if h > 1:
        take(1)
    take(0)

    for halo in halos:
        halo.wait_send()
    arrived(idsend.at[0 : nr - 1], id_send.at[0])
    for g, (p0, p1) in enumerate(spans):
        arrived(sendb.at[0 : nr - 1, p0:p1], out_send.at[g])
        arrived(backb.at[0 : nr - 1, p0:p1], ret_send.at[g])
    for one in (*hops.values(), *ghops.values()):
        one.wait_send()


def lookup(bands, found, pix, out):
    tiles = out.shape[1] // 128

    def band(i, carry):
        for j in range(tiles):
            at = slice(128 * j, 128 * j + 128)
            table = found[pl.ds(pl.multiple_of(i * (tiles * 8) + 8 * j, 8), 8), :]
            for half in range(2):
                span = pl.ds(pl.multiple_of(i * BR + 8 * half, 8), 8)
                place = swap_groups(pix[span, at])
                out[span, at] = swap_groups(jnp.take_along_axis(table, place, axis=1))
        return carry

    lax.fori_loop(0, bands, band, 0)


def per_device(nr, nz, elevation, layover, footprint_pixel, footprint_device, local_block, backscatter):
    rows, cols = elevation.shape
    tb = local_block.shape[1]
    cap = max(2, 2 * tb // (nr * nz))
    h = nz // 2
    held = backscatter.shape[0]
    vmem = pl.BlockSpec(memory_space=pltpu.VMEM)
    hbm = pl.BlockSpec(memory_space=pl.ANY)
    dma = pltpu.SemaphoreType.DMA
    gamma, found = pl.pallas_call(
        functools.partial(exchange, nr, nz, cap),
        out_shape=(
            jax.ShapeDtypeStruct((held, PIX), F32),
            jax.ShapeDtypeStruct((tb, PIX), F32),
        ),
        in_specs=[hbm, hbm, hbm, vmem, vmem, vmem],
        out_specs=(vmem, vmem),
        scratch_shapes=[
            pltpu.VMEM((rows + 16, cols + 256), F32),
            pltpu.VMEM((rows, cols), jnp.int32),
            pltpu.VMEM((rows, cols), jnp.int32),
            pltpu.VMEM((8, cols), F32),
            pltpu.VMEM((nz, 128, tb), BF16),
            pltpu.VMEM((tb, nz * 128), BF16),
            pltpu.VMEM((nz, 128, 128), BF16),
            pltpu.VMEM((nz, 128, 128), BF16),
            pltpu.VMEM((tb, PIX), F32),
            pltpu.VMEM((nr, nz, cap, PIX), F32),
            pltpu.VMEM((nr, nz, cap, PIX), F32),
            pltpu.VMEM((nr, nz, 128), F32),
            pltpu.VMEM((nr, nz, 128), F32),
            pltpu.VMEM((nz, 128, PIX), F32),
            pltpu.VMEM((2, h + 1, 2, 64, PIX), F32),
            pltpu.VMEM((2, h + 1, 2, 64, PIX), F32),
            pltpu.VMEM((nr, nz, cap, PIX), F32),
            pltpu.VMEM((nr, nz, cap, PIX), F32),
            dma((3,)),
            dma((4,)),
            dma((4,)),
            dma((1,)),
            dma((1,)),
            dma((h + 1,)),
            dma((h + 1,)),
            dma((2, h + 1, 2)),
            dma((2, h + 1, 2)),
            dma((2, h + 1, 2)),
            dma((2, h + 1, 2)),
            dma((h + 1,)),
            dma((h + 1,)),
        ],
        compiler_params=pltpu.CompilerParams(
            collective_id=0, has_side_effects=True, vmem_limit_bytes=40 * 2**20
        ),
    )(
        elevation, layover, footprint_pixel,
        footprint_device.reshape(1, tb), local_block, backscatter,
    )
    gamma_map = pl.pallas_call(
        functools.partial(lookup, rows // BR),
        out_shape=jax.ShapeDtypeStruct((rows, cols), F32),
        in_specs=[vmem, vmem],
        out_specs=vmem,
        compiler_params=pltpu.CompilerParams(vmem_limit_bytes=16 * 2**20),
    )(found, footprint_pixel)
    return gamma, gamma_map


def solution(mesh):
    in_specs = (
        P("maprow", ("mapcol", "sect")),
        P("maprow", ("mapcol", "sect")),
        P("maprow", ("mapcol", "sect")),
        P(("maprow", "mapcol", "sect"), None, None),
        P(("maprow", "mapcol", "sect"), None),
        P(("maprow", "mapcol", "sect"), None),
    )
    out_specs = (P(("maprow", "mapcol", "sect"), None), P("maprow", ("mapcol", "sect")))
    return jax.shard_map(
        functools.partial(per_device, mesh.shape["maprow"], mesh.shape["mapcol"]),
        mesh=mesh,
        in_specs=in_specs,
        out_specs=out_specs,
        check_vma=False,
    )
```

```python
import functools

import jax
import jax.numpy as jnp
from jax import lax
from jax.experimental import pallas as pl
from jax.experimental.pallas import tpu as pltpu
from jax.sharding import PartitionSpec as P

BR = 16
BC = 16
PIX = 128
CELL_SPACING = 10.0
HEADING = 0.2
MESH = pl.DeviceIdType.MESH
F32 = jnp.float32
BF16 = jnp.bfloat16


def iota(shape, dim):
    return lax.broadcasted_iota(jnp.int32, shape, dim)


def iotaf(shape, dim):
    return iota(shape, dim).astype(F32)


def swap_groups(x):
    lane, row = iota((8, 128), 1), iota((8, 128), 0)
    x = pltpu.roll(x, 0, 1, stride=16, stride_axis=0)
    x = jnp.take_along_axis(x, ((lane >> 4) - row) & 7, axis=0)
    return jnp.take_along_axis(x, (lane + 16 * row) & 127, axis=1)


def split(x):
    first = x.astype(BF16)
    return jnp.concatenate([first, (x - first.astype(F32)).astype(BF16)], axis=1)


def folded(x):
    half = x.shape[1] // 2
    return x[:, :half] + x[:, half:]


def dot(a, b):
    return lax.dot_general(a, b, (((1,), (0,)), ((), ())), preferred_element_type=F32)


def dot_nt(a, b):
    return lax.dot_general(a, b, (((1,), (1,)), ((), ())), preferred_element_type=F32)


def pixel_side(pixel):
    places = [swap_groups(pixel[8 * half : 8 * half + 8]) for half in range(2)]
    lows = [
        jnp.where((p & 15)[:, None, :] == iota((8, 16, 128), 1), 1.0, 0.0).reshape(128, 128)
        for p in places
    ]
    return jnp.concatenate(places, axis=1), jnp.concatenate(lows, axis=1).astype(BF16)


def block_sums(area, places, lows):
    firsts, seconds = [], []
    for half in range(2):
        a = swap_groups(area[8 * half : 8 * half + 8])
        high = places[:, 128 * half : 128 * half + 128] >> 4
        a1 = a.astype(BF16).astype(F32)
        a2 = a - a1
        is_high = high[:, None, :] == iota((8, 8, 128), 1)
        firsts.append(jnp.where(is_high, a1[:, None, :], 0.0).reshape(64, 128))
        seconds.append(jnp.where(is_high, a2[:, None, :], 0.0).reshape(64, 128))
    left = jnp.concatenate(
        [jnp.concatenate(firsts, axis=1), jnp.concatenate(seconds, axis=1)], axis=0
    ).astype(BF16)
    out = dot_nt(left, lows)
    out = out[:64] + out[64:]
    group = iota((8, 128), 1) >> 4
    own = out[0:8]
    for b in range(1, 8):
        own = jnp.where(group == b, out[8 * b : 8 * b + 8], own)
    return swap_groups(own)


def exchange(
    nr, nz, cap,
    elev, lay, pix, target_in, local_in, back_in,
    gamma, found, places,
    target, local, back, low_table, epad, layv, pixv, look, pmat, pmt, oht, oh, hist, sendb, recvb, idsend, idrecv,
    dense, cin, gin, backb, retb,
    in_sem, halo_send, halo_recv, id_send, id_recv, out_send, out_recv,
    chain_send, chain_recv, gchain_send, gchain_recv, ret_send, ret_recv,
):
    rows, cols = elev.shape
    tb = target_in.shape[1]
    dests = nr * nz
    h = nz // 2
    tiles = cols // 128
    r, c, s = lax.axis_index("maprow"), lax.axis_index("mapcol"), lax.axis_index("sect")
    up_z, down_z = {"mapcol": lax.rem(c + 1, nz)}, {"mapcol": lax.rem(c + nz - 1, nz)}
    west = {"mapcol": lax.rem(c + nz - 1 + s, nz), "sect": 1 - s}
    east = {"mapcol": lax.rem(c + s, nz), "sect": 1 - s}
    north, south = {"maprow": lax.rem(r + nr - 1, nr)}, {"maprow": lax.rem(r + 1, nr)}
    spans = [(0, 1)] + [(2 * g - 1, 2 * g + 1) for g in range(1, h)] + [(nz - 1, nz)]

    def place(k):
        return 2 * (k - h) if k >= h else 2 * (h - k) - 1

    barrier = pltpu.get_barrier_semaphore()

    def greet(j, carry):
        pl.semaphore_signal(
            barrier, inc=1, device_id={"maprow": lax.rem(r + j, nr)}, device_id_type=MESH
        )
        return carry

    lax.fori_loop(1, nr, greet, 0)
    for neighbour in (up_z, down_z, west, east):
        pl.semaphore_signal(barrier, inc=1, device_id=neighbour, device_id_type=MESH)

    loads = [
        pltpu.make_async_copy(target_in, target, in_sem.at[0]),
        pltpu.make_async_copy(local_in, local, in_sem.at[1]),
        pltpu.make_async_copy(pix, pixv, in_sem.at[2]),
        pltpu.make_async_copy(elev, epad.at[8 : 8 + rows, 128 : 128 + cols], in_sem.at[3]),
        pltpu.make_async_copy(lay, layv, in_sem.at[4]),
        pltpu.make_async_copy(back_in, back, in_sem.at[5]),
    ]
    for load in loads:
        load.start()

    loads[0].wait()
    loads[1].wait()
    name = target[...]
    step_z = ((name & (nz - 1)) + (nz - c)) & (nz - 1)
    ahead = step_z - h
    order = jnp.where(ahead >= 0, 2 * ahead, -2 * ahead - 1)
    spot = (name >> (nz.bit_length() - 1)) * nz + order
    onehot = iota((dests, tb), 0) == spot
    earlier = jnp.where(iota((tb, tb), 0) < iota((tb, tb), 1), 1.0, 0.0).astype(BF16)
    running = dot(jnp.where(onehot, 1.0, 0.0).astype(BF16), earlier)
    rank = jnp.sum(jnp.where(onehot, running, 0.0), axis=0, keepdims=True)
    slot = (spot * cap).astype(F32) + rank
    ids = jnp.where(onehot, local[...].astype(F32), 0.0).astype(BF16)
    at_lane = (r * cap).astype(F32) + rank
    lanes = jnp.where(iotaf((128, tb), 0) == at_lane, 1.0, 0.0).astype(BF16)
    idsend[...] = dot_nt(ids, lanes).reshape(nr, nz, 128)
    idrecv[pl.ds(r, 1)] = idsend[pl.ds(r, 1)]

    pl.semaphore_wait(barrier, nr - 1 + 4)

    halos = [
        (elev.at[rows - 8 : rows, :], epad.at[0:8, 128 : 128 + cols], south),
        (elev.at[0:8, :], epad.at[rows + 8 : rows + 16, 128 : 128 + cols], north),
        (elev.at[:, cols - 128 : cols], epad.at[8 : 8 + rows, 0:128], east),
        (elev.at[:, 0:128], epad.at[8 : 8 + rows, 128 + cols : 256 + cols], west),
    ]
    halos = [
        pltpu.make_async_remote_copy(
            src_ref=src, dst_ref=dst, send_sem=halo_send.at[i], recv_sem=halo_recv.at[i],
            device_id=where, device_id_type=MESH,
        )
        for i, (src, dst, where) in enumerate(halos)
    ]
    for halo in halos:
        halo.start()

    def to_plane(source, sink, send_sem, recv_sem):
        def body(j, carry):
            peer = lax.rem(r + j, nr)
            pltpu.make_async_remote_copy(
                src_ref=source(peer), dst_ref=sink(r), send_sem=send_sem, recv_sem=recv_sem,
                device_id={"maprow": peer}, device_id_type=MESH,
            ).start()
            return carry

        lax.fori_loop(1, nr, body, 0)

    def arrived(part, sem):
        pltpu.make_async_copy(part, part, sem).wait()

    to_plane(lambda i: idsend.at[i], lambda i: idrecv.at[i], id_send.at[0], id_recv.at[0])

    loads[2].wait()
    group_bands = 8 if rows % (8 * BR) == 0 else 2

    def pixels(i, carry):
        for n in range(group_bands):
            top = pl.multiple_of(i * (group_bands * BR) + n * BR, BR)
            for j in range(tiles):
                unit = i * (group_bands * tiles) + n * tiles + j
                place, low = pixel_side(pixv[pl.ds(top, BR), 128 * j : 128 * j + 128])
                places[pl.ds(pl.multiple_of(8 * unit, 8), 8), :] = place
                low_table[unit] = low
        return carry

    lax.fori_loop(0, rows // (group_bands * BR), pixels, 0)

    i0 = iota((128, 1), 0)
    row_slot = ((i0 // cap) * (nz * cap) + lax.rem(i0, cap)).astype(F32)
    for p in range(nz):
        pmat[p] = jnp.where(row_slot + float(p * cap) == slot, 1.0, 0.0).astype(BF16)

    column = ((c * 2 + s) * cols + iota((1, cols), 1)).astype(F32)
    incidence = 0.52 + 0.28 * (column + 0.5) / float(cols * nz * 2)
    sine, heading = jnp.sin(incidence), jnp.full((1, cols), HEADING, F32)
    look[0:1, :] = -sine * jnp.cos(heading) / (2.0 * CELL_SPACING)
    look[1:2, :] = -sine * jnp.sin(heading) / (2.0 * CELL_SPACING)
    look[2:3, :] = jnp.cos(incidence)

    loads[3].wait()
    loads[4].wait()
    for halo in halos:
        halo.wait_recv()

    @pl.when(r == 0)
    def _():
        epad[0:8, 128 : 128 + cols] = jnp.zeros((8, cols), F32)

    @pl.when(r == nr - 1)
    def _():
        epad[rows + 8 : rows + 16, 128 : 128 + cols] = jnp.zeros((8, cols), F32)

    @pl.when((c == 0) & (s == 0))
    def _():
        epad[8 : 8 + rows, 0:128] = jnp.zeros((rows, 128), F32)

    @pl.when((c == nz - 1) & (s == 1))
    def _():
        epad[8 : 8 + rows, 128 + cols : 256 + cols] = jnp.zeros((rows, 128), F32)

    def bands(i, carry):
        lane = iota((BR, 128), 1)
        for n in range(group_bands):
            top = pl.multiple_of(i * (group_bands * BR) + n * BR, BR)
            around = epad[pl.ds(top, 32), 128 : 128 + cols]
            mid = epad[pl.ds(pl.multiple_of(top + 8, 8), BR), :]
            mids = [mid[:, 128 * j : 128 * j + 128] for j in range(tiles + 2)]
            right = [pltpu.roll(x, 1, 1) for x in mids[:-1]]
            left = [pltpu.roll(x, 127, 1) for x in mids[1:]]
            for j in range(tiles):
                at = slice(128 * j, 128 * j + 128)
                unit = i * (group_bands * tiles) + n * tiles + j
                span = pl.ds(pl.multiple_of(8 * unit, 8), 8)
                before = jnp.where(lane == 0, right[j], right[j + 1])
                after = jnp.where(lane == 127, left[j + 1], left[j])
                rise_cols = after - before
                rise_rows = around[9:25, at] - around[7:23, at]
                facing = (
                    look[2:3, at] - rise_cols * look[0:1, at] - rise_rows * look[1:2, at]
                )
                lit = (1 - layv[pl.ds(top, BR), at]).astype(F32)
                area = jnp.maximum(facing, 0.0) * lit
                hist[span, :] = block_sums(area, places[span, :], low_table[unit])
        return carry

    lax.fori_loop(0, rows // (group_bands * BR), bands, 0)

    terms = split(hist[...])
    for g, (p0, p1) in enumerate(spans):
        for p in range(p0, p1):
            sendb[:, p] = folded(dot(pmat[p], terms)).reshape(nr, cap, PIX)
        recvb[pl.ds(r, 1), p0:p1] = sendb[pl.ds(r, 1), p0:p1]
        to_plane(
            lambda i: sendb.at[i, p0:p1], lambda i: recvb.at[i, p0:p1],
            out_send.at[g], out_recv.at[g],
        )

    i1 = iota((1, 128), 1)
    lane_slot = ((i1 // cap) * (nz * cap) + lax.rem(i1, cap)).astype(F32)
    slot_down = jnp.transpose(jnp.broadcast_to(slot, (128, tb)))
    for p in range(nz):
        pmt[:, 128 * p : 128 * p + 128] = jnp.where(
            slot_down == lane_slot + float(p * cap), 1.0, 0.0
        ).astype(BF16)

    loads[5].wait()
    arrived(idrecv.at[0 : nr - 1], id_recv.at[0])
    names = idrecv[0]
    for i in range(1, nr):
        names = names + idrecv[i]
    for p in range(nz):
        wide = jnp.broadcast_to(names[p : p + 1, :], (128, 128))
        oht[p] = jnp.where(wide == iotaf((128, 128), 0), 1.0, 0.0).astype(BF16)
        oh[p] = jnp.where(jnp.transpose(wide) == iotaf((128, 128), 1), 1.0, 0.0).astype(BF16)

    def hop(source, sinks, sends, recvs, way, j, q):
        return pltpu.make_async_remote_copy(
            src_ref=source, dst_ref=sinks.at[way, j, q],
            send_sem=sends.at[way, j, q], recv_sem=recvs.at[way, j, q],
            device_id=(up_z, down_z)[way], device_id_type=MESH,
        )

    def pieces(j, last):
        if j == last:
            return [(0, 0), (1, 1)]
        return [(w, q) for q in range(2) for w in range(2)]

    hops = {}
    for g, (p0, p1) in enumerate(spans):
        arrived(recvb.at[0 : nr - 1, p0:p1], out_recv.at[g])
        for p in range(p0, p1):
            dense[p] = folded(dot(oht[p], split(recvb[:, p].reshape(128, PIX))))
        if g < h:
            for way, q in pieces(g + 1, 1):
                p = place(h - g if way == 0 else h + g)
                part = slice(64 * q, 64 * q + 64)
                if (way, g, q) in hops:
                    hops[way, g, q].wait_recv()
                    dense[p, part] = dense[p, part] + cin[way, g, q]
                hops[way, g + 1, q] = hop(
                    dense.at[p, part], cin, chain_send, chain_recv, way, g + 1, q
                )
                hops[way, g + 1, q].start()
        else:
            for q in range(2):
                part = slice(64 * q, 64 * q + 64)
                total = dense[p0, part]
                for way in range(2):
                    if (way, g, q) in hops:
                        hops[way, g, q].wait_recv()
                        total = total + cin[way, g, q]
                gamma[part] = back[part] / jnp.maximum(total, 1.0)

    ghops = {}

    def pass_on(j):
        for way, q in pieces(j, h):
            source = gamma.at[64 * q : 64 * q + 64] if j == 1 else gin.at[way, j - 1, q]
            if j > 1:
                ghops[way, j - 1, q].wait_recv()
            ghops[way, j, q] = hop(source, gin, gchain_send, gchain_recv, way, j, q)
            ghops[way, j, q].start()

    def give(g, tables):
        p0, p1 = spans[g]
        for p, table in zip(range(p0, p1), tables):
            backb[:, p] = folded(dot(oh[p], split(table))).reshape(nr, cap, PIX)
        retb[pl.ds(r, 1), p0:p1] = backb[pl.ds(r, 1), p0:p1]
        to_plane(
            lambda i: backb.at[i, p0:p1], lambda i: retb.at[i, p0:p1],
            ret_send.at[g], ret_recv.at[g],
        )

    def take(g):
        p0, p1 = spans[g]
        arrived(retb.at[0 : nr - 1, p0:p1], ret_recv.at[g])
        given = jnp.concatenate(
            [split(retb[:, p].reshape(128, PIX)) for p in range(p0, p1)], axis=0
        )
        rows_found = folded(dot(pmt[:, 128 * p0 : 128 * p1], given))
        found[...] = rows_found if g == h else found[...] + rows_found

    pass_on(1)
    give(h, [gamma[...]])
    for j in range(1, h):
        pass_on(j + 1)
        for way, q in pieces(j, h):
            if (way, j + 1, q) not in ghops:
                ghops[way, j, q].wait_recv()
        give(h - j, [gin[1, j].reshape(128, PIX), gin[0, j].reshape(128, PIX)])
        take(h - j + 1)
    for way, q in pieces(h, h):
        ghops[way, h, q].wait_recv()
    give(0, [jnp.concatenate([gin[0, h, 0], gin[1, h, 1]], axis=0)])
    if h > 1:
        take(1)
    take(0)

    for halo in halos:
        halo.wait_send()
    arrived(idsend.at[0 : nr - 1], id_send.at[0])
    for g, (p0, p1) in enumerate(spans):
        arrived(sendb.at[0 : nr - 1, p0:p1], out_send.at[g])
        arrived(backb.at[0 : nr - 1, p0:p1], ret_send.at[g])
    for one in (*hops.values(), *ghops.values()):
        one.wait_send()


def lookup(found, places, gamma, gamma_out, out, cells, sems):
    rows, cols = out.shape
    tiles = cols // 128
    chunk = 64 if rows % 64 == 0 else rows
    copies = [pltpu.make_async_copy(gamma, gamma_out, sems.at[0])]
    copies[0].start()
    for k in range(rows // chunk):
        for i in range(k * (chunk // BR), (k + 1) * (chunk // BR)):
            for j in range(tiles):
                span = slice(8 * (i * tiles + j), 8 * (i * tiles + j) + 8)
                for half in range(2):
                    place = places[span, 128 * half : 128 * half + 128]
                    value = jnp.take_along_axis(found[span, :], place, axis=1)
                    top = BR * i + 8 * half
                    cells[top : top + 8, 128 * j : 128 * j + 128] = swap_groups(value)
        part = slice(k * chunk, (k + 1) * chunk)
        copies.append(pltpu.make_async_copy(cells.at[part], out.at[part], sems.at[k + 1]))
        copies[-1].start()
    for copy in copies:
        copy.wait()


def per_device(nr, nz, elevation, layover, footprint_pixel, footprint_device, local_block, backscatter):
    rows, cols = elevation.shape
    tb = local_block.shape[1]
    cap = max(2, 2 * tb // (nr * nz))
    h = nz // 2
    held = backscatter.shape[0]
    vmem = pl.BlockSpec(memory_space=pltpu.VMEM)
    hbm = pl.BlockSpec(memory_space=pltpu.HBM)
    dma = pltpu.SemaphoreType.DMA
    gamma, found, places = pl.pallas_call(
        functools.partial(exchange, nr, nz, cap),
        out_shape=(
            jax.ShapeDtypeStruct((held, PIX), F32),
            jax.ShapeDtypeStruct((tb, PIX), F32),
            jax.ShapeDtypeStruct((tb, BR * BC), jnp.int32),
        ),
        in_specs=[hbm] * 6,
        out_specs=(vmem, vmem, vmem),
        scratch_shapes=[
            pltpu.VMEM((1, tb), jnp.int32),
            pltpu.VMEM((1, tb), jnp.int32),
            pltpu.VMEM((held, PIX), F32),
            pltpu.VMEM((tb // 8, 128, BR * BC), BF16),
            pltpu.VMEM((rows + 16, cols + 256), F32),
            pltpu.VMEM((rows, cols), jnp.int32),
            pltpu.VMEM((rows, cols), jnp.int32),
            pltpu.VMEM((8, cols), F32),
            pltpu.VMEM((nz, 128, tb), BF16),
            pltpu.VMEM((tb, nz * 128), BF16),
            pltpu.VMEM((nz, 128, 128), BF16),
            pltpu.VMEM((nz, 128, 128), BF16),
            pltpu.VMEM((tb, PIX), F32),
            pltpu.VMEM((nr, nz, cap, PIX), F32),
            pltpu.VMEM((nr, nz, cap, PIX), F32),
            pltpu.VMEM((nr, nz, 128), F32),
            pltpu.VMEM((nr, nz, 128), F32),
            pltpu.VMEM((nz, 128, PIX), F32),
            pltpu.VMEM((2, h + 1, 2, 64, PIX), F32),
            pltpu.VMEM((2, h + 1, 2, 64, PIX), F32),
            pltpu.VMEM((nr, nz, cap, PIX), F32),
            pltpu.VMEM((nr, nz, cap, PIX), F32),
            dma((6,)),
            dma((4,)),
            dma((4,)),
            dma((1,)),
            dma((1,)),
            dma((h + 1,)),
            dma((h + 1,)),
            dma((2, h + 1, 2)),
            dma((2, h + 1, 2)),
            dma((2, h + 1, 2)),
            dma((2, h + 1, 2)),
            dma((h + 1,)),
            dma((h + 1,)),
        ],
        compiler_params=pltpu.CompilerParams(
            collective_id=0, has_side_effects=True, vmem_limit_bytes=40 * 2**20
        ),
    )(
        *(
            pltpu.with_memory_space_constraint(x, pltpu.HBM)
            for x in (
                elevation, layover, footprint_pixel,
                footprint_device.reshape(1, tb), local_block, backscatter,
            )
        )
    )
    return pl.pallas_call(
        lookup,
        out_shape=(
            jax.ShapeDtypeStruct((held, PIX), F32),
            jax.ShapeDtypeStruct((rows, cols), F32),
        ),
        in_specs=[vmem, vmem, vmem],
        out_specs=(hbm, hbm),
        scratch_shapes=[pltpu.VMEM((rows, cols), F32), dma((1 + max(1, rows // 64),))],
        compiler_params=pltpu.CompilerParams(vmem_limit_bytes=8 * 2**20),
    )(found, places, gamma)


def solution(mesh):
    in_specs = (
        P("maprow", ("mapcol", "sect")),
        P("maprow", ("mapcol", "sect")),
        P("maprow", ("mapcol", "sect")),
        P(("maprow", "mapcol", "sect"), None, None),
        P(("maprow", "mapcol", "sect"), None),
        P(("maprow", "mapcol", "sect"), None),
    )
    out_specs = (P(("maprow", "mapcol", "sect"), None), P("maprow", ("mapcol", "sect")))
    return jax.shard_map(
        functools.partial(per_device, mesh.shape["maprow"], mesh.shape["mapcol"]),
        mesh=mesh,
        in_specs=in_specs,
        out_specs=out_specs,
        check_vma=False,
    )
```

```python
import functools

import jax
import jax.numpy as jnp
from jax import lax
from jax.experimental import pallas as pl
from jax.experimental.pallas import tpu as pltpu
from jax.sharding import PartitionSpec as P

BR = 16
BC = 16
PIX = 128
CELL_SPACING = 10.0
HEADING = 0.2
MESH = pl.DeviceIdType.MESH
F32 = jnp.float32
BF16 = jnp.bfloat16


def iota(shape, dim):
    return lax.broadcasted_iota(jnp.int32, shape, dim)


def iotaf(shape, dim):
    return iota(shape, dim).astype(F32)


def swap_groups(x):
    lane, row = iota((8, 128), 1), iota((8, 128), 0)
    x = pltpu.roll(x, 0, 1, stride=16, stride_axis=0)
    x = jnp.take_along_axis(x, ((lane >> 4) - row) & 7, axis=0)
    return jnp.take_along_axis(x, (lane + 16 * row) & 127, axis=1)


def split(x):
    first = x.astype(BF16)
    return jnp.concatenate([first, (x - first.astype(F32)).astype(BF16)], axis=1)


def folded(x):
    half = x.shape[1] // 2
    return x[:, :half] + x[:, half:]


def dot(a, b):
    return lax.dot_general(a, b, (((1,), (0,)), ((), ())), preferred_element_type=F32)


def dot_nt(a, b):
    return lax.dot_general(a, b, (((1,), (1,)), ((), ())), preferred_element_type=F32)


def pixel_side(pixel):
    places = [swap_groups(pixel[8 * half : 8 * half + 8]) for half in range(2)]
    lows = [
        jnp.where((p & 15)[:, None, :] == iota((8, 16, 128), 1), 1.0, 0.0).reshape(128, 128)
        for p in places
    ]
    return jnp.concatenate(places, axis=1), jnp.concatenate(lows, axis=1).astype(BF16)


def block_sums(area, places, lows):
    firsts, seconds = [], []
    for half in range(2):
        a = swap_groups(area[8 * half : 8 * half + 8])
        high = places[:, 128 * half : 128 * half + 128] >> 4
        a1 = a.astype(BF16).astype(F32)
        a2 = a - a1
        is_high = high[:, None, :] == iota((8, 8, 128), 1)
        firsts.append(jnp.where(is_high, a1[:, None, :], 0.0).reshape(64, 128))
        seconds.append(jnp.where(is_high, a2[:, None, :], 0.0).reshape(64, 128))
    left = jnp.concatenate(
        [jnp.concatenate(firsts, axis=1), jnp.concatenate(seconds, axis=1)], axis=0
    ).astype(BF16)
    out = dot_nt(left, lows)
    out = out[:64] + out[64:]
    group = iota((8, 128), 1) >> 4
    own = out[0:8]
    for b in range(1, 8):
        own = jnp.where(group == b, out[8 * b : 8 * b + 8], own)
    return swap_groups(own)


STEP = (0, 2, -2, 1, 3, -1, -3, 4)
SPANS = ((3, 5, 1), (5, 7, -1), (7, 8, 2), (0, 3, 0))
TABLES = ((1, 4, 7), (2, 6, 7), (0, 3, 5))


def exchange(
    nr, nz, cap,
    elev, lay, pix, target_in, local_in, back_in,
    gamma, found, places,
    target, local, back, low_table, epad, layv, pixv, look, put_low, put_high, pick, oht, oh, hist,
    sendb, recvb, idsend, idrecv, partial, cin, packed, gin, backb, retb,
    in_sem, halo_send, halo_recv, id_send, id_recv, out_send, out_recv,
    sum_send, sum_recv, gam_send, gam_recv, ret_send, ret_recv,
):
    rows, cols = elev.shape
    tb = target_in.shape[1]
    dests = nr * nz
    hc = cap // 2
    n4 = nr * hc
    tiles = cols // 128
    r, c, s = lax.axis_index("maprow"), lax.axis_index("mapcol"), lax.axis_index("sect")

    def plane(step):
        return lax.rem(c + (step + nz), nz)

    west = {"mapcol": lax.rem(c + nz - 1 + s, nz), "sect": 1 - s}
    east = {"mapcol": lax.rem(c + s, nz), "sect": 1 - s}
    north, south = {"maprow": lax.rem(r + nr - 1, nr)}, {"maprow": lax.rem(r + 1, nr)}

    barrier = pltpu.get_barrier_semaphore()

    def greet(j, carry):
        peer = lax.rem(r + j, nr)
        for step in (1, -1, 2, -2):
            pl.semaphore_signal(
                barrier, inc=1, device_id={"maprow": peer, "mapcol": plane(step)},
                device_id_type=MESH,
            )
        return carry

    def greet_plane(j, carry):
        pl.semaphore_signal(
            barrier, inc=1, device_id={"maprow": lax.rem(r + j, nr)}, device_id_type=MESH
        )
        return carry

    for neighbour in (west, east):
        pl.semaphore_signal(barrier, inc=1, device_id=neighbour, device_id_type=MESH)
    lax.fori_loop(1, nr, greet_plane, 0)
    lax.fori_loop(0, nr, greet, 0)

    loads = [
        pltpu.make_async_copy(target_in, target, in_sem.at[0]),
        pltpu.make_async_copy(local_in, local, in_sem.at[1]),
        pltpu.make_async_copy(pix, pixv, in_sem.at[2]),
        pltpu.make_async_copy(elev, epad.at[8 : 8 + rows, 128 : 128 + cols], in_sem.at[3]),
        pltpu.make_async_copy(lay, layv, in_sem.at[4]),
        pltpu.make_async_copy(back_in, back, in_sem.at[5]),
    ]
    for load in loads:
        load.start()

    loads[0].wait()
    loads[1].wait()
    name = target[...]
    ahead = ((name & (nz - 1)) + (nz - c)) & (nz - 1)
    order = jnp.zeros((1, tb), jnp.int32)
    for p, step in enumerate(STEP):
        order = jnp.where(ahead == step % nz, p, order)
    spot = (name >> (nz.bit_length() - 1)) * nz + order
    onehot = iota((dests, tb), 0) == spot
    earlier = jnp.where(iota((tb, tb), 0) < iota((tb, tb), 1), 1.0, 0.0).astype(BF16)
    running = dot(jnp.where(onehot, 1.0, 0.0).astype(BF16), earlier)
    rank = jnp.sum(jnp.where(onehot, running, 0.0), axis=0, keepdims=True)
    slot = (spot * cap).astype(F32) + rank
    ids = jnp.where(onehot, local[...].astype(F32), 0.0).astype(BF16)
    high = rank >= float(hc)
    within = jnp.where(high, rank - float(hc), rank)
    at_lane = (r * hc).astype(F32) + within + jnp.where(high, float(n4), 0.0)
    lanes = jnp.where(iotaf((128, tb), 0) == at_lane, 1.0, 0.0).astype(BF16)
    idsend[...] = dot_nt(ids, lanes).reshape(nr, nz, 128)
    idrecv[pl.ds(r, 1), 0:3] = idsend[pl.ds(r, 1), 0:3]

    pl.semaphore_wait(barrier, 5 * nr - 1 + 2)

    halos = [
        (elev.at[rows - 8 : rows, :], epad.at[0:8, 128 : 128 + cols], south),
        (elev.at[0:8, :], epad.at[rows + 8 : rows + 16, 128 : 128 + cols], north),
        (elev.at[:, cols - 128 : cols], epad.at[8 : 8 + rows, 0:128], east),
        (elev.at[:, 0:128], epad.at[8 : 8 + rows, 128 + cols : 256 + cols], west),
    ]
    halos = [
        pltpu.make_async_remote_copy(
            src_ref=src, dst_ref=dst, send_sem=halo_send.at[i], recv_sem=halo_recv.at[i],
            device_id=where, device_id_type=MESH,
        )
        for i, (src, dst, where) in enumerate(halos)
    ]
    for halo in halos:
        halo.start()

    def to_peers(source, sink, send_sem, recv_sem, way):
        def start(span, peer):
            p0, p1, step = span
            where = plane(way * step)
            if step == 2:
                where = jnp.where((r + peer) % 2 == 0, plane(2 * way), plane(-2 * way))
            k = 0 if step == 0 else 1
            pltpu.make_async_remote_copy(
                src_ref=source(p0, p1, peer), dst_ref=sink(p0, p1, r),
                send_sem=send_sem.at[k], recv_sem=recv_sem.at[k],
                device_id={"maprow": peer, "mapcol": where}, device_id_type=MESH,
            ).start()

        def far(j, carry):
            for span in SPANS[:3]:
                start(span, lax.rem(r + j, nr))
            return carry

        def near(j, carry):
            start(SPANS[3], lax.rem(r + j, nr))
            return carry

        lax.fori_loop(0, nr, far, 0)
        lax.fori_loop(1, nr, near, 0)

    def done(part, sem):
        pltpu.make_async_copy(part, part, sem).wait()

    def done_rows(buffer, sem):
        done(buffer.at[3:nz], sem.at[1])
        done(buffer.at[0:3, 0 : (nr - 1) * hc], sem.at[0])

    def of_rows(buffer):
        return lambda p0, p1, i: buffer.at[p0:p1, pl.ds(i * hc, hc)]

    to_peers(
        lambda p0, p1, i: idsend.at[i, p0:p1], lambda p0, p1, i: idrecv.at[i, p0:p1],
        id_send, id_recv, 1,
    )

    loads[2].wait()
    group_bands = 8 if rows % (8 * BR) == 0 else 2

    def pixels(i, carry):
        for n in range(group_bands):
            top = pl.multiple_of(i * (group_bands * BR) + n * BR, BR)
            for j in range(tiles):
                unit = i * (group_bands * tiles) + n * tiles + j
                place, low = pixel_side(pixv[pl.ds(top, BR), 128 * j : 128 * j + 128])
                places[pl.ds(pl.multiple_of(8 * unit, 8), 8), :] = place
                low_table[unit] = low
        return carry

    lax.fori_loop(0, rows // (group_bands * BR), pixels, 0)

    i0 = iota((nz * n4, 1), 0)
    row_slot = (((i0 % n4) // hc) * (nz * cap) + (i0 // n4) * cap + i0 % hc).astype(F32)
    put_low[...] = jnp.where(row_slot == slot, 1.0, 0.0).astype(BF16)
    put_high[...] = jnp.where(row_slot + float(hc) == slot, 1.0, 0.0).astype(BF16)

    column = ((c * 2 + s) * cols + iota((1, cols), 1)).astype(F32)
    incidence = 0.52 + 0.28 * (column + 0.5) / float(cols * nz * 2)
    sine, heading = jnp.sin(incidence), jnp.full((1, cols), HEADING, F32)
    look[0:1, :] = -sine * jnp.cos(heading) / (2.0 * CELL_SPACING)
    look[1:2, :] = -sine * jnp.sin(heading) / (2.0 * CELL_SPACING)
    look[2:3, :] = jnp.cos(incidence)

    loads[3].wait()
    loads[4].wait()
    for halo in halos:
        halo.wait_recv()

    @pl.when(r == 0)
    def _():
        epad[0:8, 128 : 128 + cols] = jnp.zeros((8, cols), F32)

    @pl.when(r == nr - 1)
    def _():
        epad[rows + 8 : rows + 16, 128 : 128 + cols] = jnp.zeros((8, cols), F32)

    @pl.when((c == 0) & (s == 0))
    def _():
        epad[8 : 8 + rows, 0:128] = jnp.zeros((rows, 128), F32)

    @pl.when((c == nz - 1) & (s == 1))
    def _():
        epad[8 : 8 + rows, 128 + cols : 256 + cols] = jnp.zeros((rows, 128), F32)

    def bands(i, carry):
        lane = iota((BR, 128), 1)
        for n in range(group_bands):
            top = pl.multiple_of(i * (group_bands * BR) + n * BR, BR)
            around = epad[pl.ds(top, 32), 128 : 128 + cols]
            mid = epad[pl.ds(pl.multiple_of(top + 8, 8), BR), :]
            mids = [mid[:, 128 * j : 128 * j + 128] for j in range(tiles + 2)]
            right = [pltpu.roll(x, 1, 1) for x in mids[:-1]]
            left = [pltpu.roll(x, 127, 1) for x in mids[1:]]
            for j in range(tiles):
                at = slice(128 * j, 128 * j + 128)
                unit = i * (group_bands * tiles) + n * tiles + j
                span = pl.ds(pl.multiple_of(8 * unit, 8), 8)
                before = jnp.where(lane == 0, right[j], right[j + 1])
                after = jnp.where(lane == 127, left[j + 1], left[j])
                rise_cols = after - before
                rise_rows = around[9:25, at] - around[7:23, at]
                facing = (
                    look[2:3, at] - rise_cols * look[0:1, at] - rise_rows * look[1:2, at]
                )
                lit = (1 - layv[pl.ds(top, BR), at]).astype(F32)
                area = jnp.maximum(facing, 0.0) * lit
                hist[span, :] = block_sums(area, places[span, :], low_table[unit])
        return carry

    lax.fori_loop(0, rows // (group_bands * BR), bands, 0)

    left = iota((nz * n4, 128), 1) < 64
    sums = hist[...]
    lower = folded(dot(put_low[...], split(sums)))
    upper = folded(dot(put_high[...], split(pltpu.roll(sums, 64, 1))))
    sendb[0] = jnp.where(left, lower, upper).reshape(nz, n4, 128)
    sendb[1] = jnp.where(left, upper, lower).reshape(nz, n4, 128)
    mine = pl.ds(r * hc, hc)
    for q in range(2):
        recvb[q, 0:3, mine] = sendb[q, 0:3, mine]
        to_peers(of_rows(sendb.at[q]), of_rows(recvb.at[q]), out_send.at[q], out_recv.at[q], 1)

    row_of = (
        within
        + (((spot & (nz - 1)) * nr + (spot >> (nz.bit_length() - 1))) * hc).astype(F32)
        + jnp.where(high, float(nz * n4), 0.0)
    )
    row_down = jnp.transpose(jnp.broadcast_to(row_of, (128, tb)))
    high_down = row_down >= float(nz * n4)
    row_down = jnp.where(high_down, row_down - float(nz * n4), row_down)
    for n in range(0, nz * n4, 128):
        width = min(128, nz * n4 - n)
        pick[:, n : n + width] = jnp.where(
            row_down[:, :width] == iotaf((1, width), 1) + float(n), 1.0, 0.0
        ).astype(BF16)

    loads[5].wait()
    done(idrecv.at[:, 3:nz], id_recv.at[1])
    done(idrecv.at[0 : nr - 1, 0:3], id_recv.at[0])
    names = idrecv[0]
    for i in range(1, nr):
        names = names + idrecv[i]
    lane = iota((1, 128), 1)
    even = ((lane % n4) // hc + r) % 2 == 0
    for t, table in enumerate(TABLES):
        for m, p in enumerate(table):
            name = names[p : p + 1, :]
            if p == 7:
                name = jnp.where(even == (t == 0), name, -1.0)
            if 2 * n4 < 128:
                name = jnp.where(lane < 2 * n4, name, -1.0)
            wide = jnp.broadcast_to(name, (128, 128))
            at = slice(128 * m, 128 * m + 128)
            oht[t, :, at] = jnp.where(wide == iotaf((128, 128), 0), 1.0, 0.0).astype(BF16)
            oh[t, at, :] = jnp.where(
                jnp.transpose(wide) == iotaf((128, 128), 1), 1.0, 0.0
            ).astype(BF16)
    half = iota((64, 128), 1) < 64
    backs = [back[0:64, :], back[64:128, :]]
    backs = [
        jnp.where(half, backs[0], pltpu.roll(backs[1], 64, 1)),
        jnp.where(half, pltpu.roll(backs[0], 64, 1), backs[1]),
    ]

    def filled(x):
        if 2 * n4 == 128:
            return x
        return jnp.concatenate([x, jnp.zeros((128 - 2 * n4, 128), F32)], axis=0)

    def table_of(q, t):
        given = []
        for p in TABLES[t]:
            x = recvb[q, p]
            y = pltpu.roll(x, 64, 1)
            given.append(split(filled(jnp.concatenate([x, y] if q == 0 else [y, x], axis=0))))
        total = folded(dot(oht[t], jnp.concatenate(given, axis=0)))
        return jnp.where(half, total[0:64], pltpu.roll(total[64:128], 64, 1))

    def two_steps(source, sink, send_sem, recv_sem, way):
        return pltpu.make_async_remote_copy(
            src_ref=source, dst_ref=sink.at[way],
            send_sem=send_sem.at[way], recv_sem=recv_sem.at[way],
            device_id={"mapcol": plane((2, -2)[way])}, device_id_type=MESH,
        )

    hops = []
    own = []
    for q in range(2):
        done_rows(recvb.at[q], out_recv.at[q])
        for way in range(2):
            partial[q, way] = table_of(q, way)
            hops.append(
                two_steps(partial.at[q, way], cin.at[q], sum_send.at[q], sum_recv.at[q], way)
            )
            hops[-1].start()
        own.append(table_of(q, 2))
    gammas = []
    for q in range(2):
        hops[2 * q].wait_recv()
        hops[2 * q + 1].wait_recv()
        total = own[q] + cin[q, 0] + cin[q, 1]
        packed[q] = backs[q] / jnp.maximum(total, 1.0)
        for way in range(2):
            gammas.append(
                two_steps(packed.at[q], gin.at[q], gam_send.at[q], gam_recv.at[q], way)
            )
            gammas[-1].start()
    halves = [(packed[q], pltpu.roll(packed[q], 64, 1)) for q in range(2)]
    gamma[0:64] = jnp.where(half, halves[0][0], halves[1][1])
    gamma[64:128] = jnp.where(half, halves[0][1], halves[1][0])

    def served(q, t):
        x = packed[q] if t == 2 else gin[q, 1 - t]
        y = pltpu.roll(x, 64, 1)
        whole = jnp.concatenate([jnp.where(half, x, y), jnp.where(half, y, x)], axis=0)
        asked = folded(dot(oh[t], split(whole)))
        slots = iota((n4, 128), 1) < 64
        return [
            jnp.where(
                slots, asked[128 * m : 128 * m + n4], asked[128 * m + n4 : 128 * m + 2 * n4]
            )
            for m in range(3)
        ]

    for q in range(2):
        for p, x in zip(TABLES[2], served(q, 2)):
            backb[q, p] = x
        gammas[2 * q].wait_recv()
        gammas[2 * q + 1].wait_recv()
        ahead_rows, behind_rows = served(q, 0), served(q, 1)
        backb[q, 1], backb[q, 4] = ahead_rows[0], ahead_rows[1]
        backb[q, 2], backb[q, 6] = behind_rows[0], behind_rows[1]
        backb[q, 7] = ahead_rows[2] + behind_rows[2]
        retb[q, 0:3, mine] = backb[q, 0:3, mine]
        to_peers(of_rows(backb.at[q]), of_rows(retb.at[q]), ret_send.at[q], ret_recv.at[q], -1)

    left = iota((tb, 128), 1) < 64
    for q in range(2):
        done_rows(retb.at[q], ret_recv.at[q])
        x = folded(dot(pick[...], split(retb[q].reshape(nz * n4, 128))))
        y = pltpu.roll(x, 64, 1)
        if q == 0:
            found[...] = jnp.where(high_down, y, x)
        else:
            found[...] = jnp.where(left, found[...], jnp.where(high_down, x, y))

    for halo in halos:
        halo.wait_send()
    done(idsend.at[:, 3:nz], id_send.at[1])
    done(idsend.at[0 : nr - 1, 0:3], id_send.at[0])
    for q in range(2):
        done_rows(sendb.at[q], out_send.at[q])
        done_rows(backb.at[q], ret_send.at[q])
    for one in (*hops, *gammas):
        one.wait_send()


def lookup(found, places, gamma, gamma_out, out, cells, sems):
    rows, cols = out.shape
    tiles = cols // 128
    chunk = 64 if rows % 64 == 0 else rows
    copies = [pltpu.make_async_copy(gamma, gamma_out, sems.at[0])]
    copies[0].start()
    for unit in range(rows // BR * tiles):
        span = slice(8 * unit, 8 * unit + 8)
        for half in range(2):
            place = places[span, 128 * half : 128 * half + 128]
            top, at = BR * (unit // tiles) + 8 * half, 128 * (unit % tiles)
            cells[top : top + 8, at : at + 128] = jnp.take_along_axis(
                found[span, :], place, axis=1
            )
    for k in range(rows // chunk):
        for top in range(k * chunk, (k + 1) * chunk, 8):
            for at in range(0, cols, 128):
                piece = (slice(top, top + 8), slice(at, at + 128))
                cells[piece] = swap_groups(cells[piece])
        part = slice(k * chunk, (k + 1) * chunk)
        copies.append(pltpu.make_async_copy(cells.at[part], out.at[part], sems.at[k + 1]))
        copies[-1].start()
    for copy in copies:
        copy.wait()


def per_device(nr, nz, elevation, layover, footprint_pixel, footprint_device, local_block, backscatter):
    rows, cols = elevation.shape
    tb = local_block.shape[1]
    cap = max(2, 2 * tb // (nr * nz))
    n4 = nr * cap // 2
    held = backscatter.shape[0]
    vmem = pl.BlockSpec(memory_space=pltpu.VMEM)
    hbm = pl.BlockSpec(memory_space=pltpu.HBM)
    dma = pltpu.SemaphoreType.DMA
    gamma, found, places = pl.pallas_call(
        functools.partial(exchange, nr, nz, cap),
        out_shape=(
            jax.ShapeDtypeStruct((held, PIX), F32),
            jax.ShapeDtypeStruct((tb, PIX), F32),
            jax.ShapeDtypeStruct((tb, BR * BC), jnp.int32),
        ),
        in_specs=[hbm] * 6,
        out_specs=(vmem, vmem, vmem),
        scratch_shapes=[
            pltpu.VMEM((1, tb), jnp.int32),
            pltpu.VMEM((1, tb), jnp.int32),
            pltpu.VMEM((held, PIX), F32),
            pltpu.VMEM((tb // 8, 128, BR * BC), BF16),
            pltpu.VMEM((rows + 16, cols + 256), F32),
            pltpu.VMEM((rows, cols), jnp.int32),
            pltpu.VMEM((rows, cols), jnp.int32),
            pltpu.VMEM((8, cols), F32),
            pltpu.VMEM((nz * n4, tb), BF16),
            pltpu.VMEM((nz * n4, tb), BF16),
            pltpu.VMEM((tb, nz * n4), BF16),
            pltpu.VMEM((3, 128, 3 * 128), BF16),
            pltpu.VMEM((3, 3 * 128, 128), BF16),
            pltpu.VMEM((tb, PIX), F32),
            pltpu.VMEM((2, nz, n4, 128), F32),
            pltpu.VMEM((2, nz, n4, 128), F32),
            pltpu.VMEM((nr, nz, 128), F32),
            pltpu.VMEM((nr, nz, 128), F32),
            pltpu.VMEM((2, 2, 64, 128), F32),
            pltpu.VMEM((2, 2, 64, 128), F32),
            pltpu.VMEM((2, 64, 128), F32),
            pltpu.VMEM((2, 2, 64, 128), F32),
            pltpu.VMEM((2, nz, n4, 128), F32),
            pltpu.VMEM((2, nz, n4, 128), F32),
            dma((6,)),
            dma((4,)),
            dma((4,)),
            dma((2,)),
            dma((2,)),
            *([dma((2, 2))] * 8),
        ],
        compiler_params=pltpu.CompilerParams(
            collective_id=0, has_side_effects=True, vmem_limit_bytes=40 * 2**20
        ),
    )(
        *(
            pltpu.with_memory_space_constraint(x, pltpu.HBM)
            for x in (
                elevation, layover, footprint_pixel,
                footprint_device.reshape(1, tb), local_block, backscatter,
            )
        )
    )
    return pl.pallas_call(
        lookup,
        out_shape=(
            jax.ShapeDtypeStruct((held, PIX), F32),
            jax.ShapeDtypeStruct((rows, cols), F32),
        ),
        in_specs=[vmem, vmem, vmem],
        out_specs=(hbm, hbm),
        scratch_shapes=[pltpu.VMEM((rows, cols), F32), dma((1 + max(1, rows // 64),))],
        compiler_params=pltpu.CompilerParams(vmem_limit_bytes=8 * 2**20),
    )(found, places, gamma)


def solution(mesh):
    in_specs = (
        P("maprow", ("mapcol", "sect")),
        P("maprow", ("mapcol", "sect")),
        P("maprow", ("mapcol", "sect")),
        P(("maprow", "mapcol", "sect"), None, None),
        P(("maprow", "mapcol", "sect"), None),
        P(("maprow", "mapcol", "sect"), None),
    )
    out_specs = (P(("maprow", "mapcol", "sect"), None), P("maprow", ("mapcol", "sect")))
    return jax.shard_map(
        functools.partial(per_device, mesh.shape["maprow"], mesh.shape["mapcol"]),
        mesh=mesh,
        in_specs=in_specs,
        out_specs=out_specs,
        check_vma=False,
    )
```

```python
import functools

import jax
import jax.numpy as jnp
from jax import lax
from jax.experimental import pallas as pl
from jax.experimental.pallas import tpu as pltpu
from jax.sharding import PartitionSpec as P

BR = 16
BC = 16
PIX = 128
CELL_SPACING = 10.0
HEADING = 0.2
MESH = pl.DeviceIdType.MESH
F32 = jnp.float32
BF16 = jnp.bfloat16


def iota(shape, dim):
    return lax.broadcasted_iota(jnp.int32, shape, dim)


def iotaf(shape, dim):
    return iota(shape, dim).astype(F32)


def swap_groups(x):
    lane, row = iota((8, 128), 1), iota((8, 128), 0)
    x = pltpu.roll(x, 0, 1, stride=16, stride_axis=0)
    x = jnp.take_along_axis(x, ((lane >> 4) - row) & 7, axis=0)
    return jnp.take_along_axis(x, (lane + 16 * row) & 127, axis=1)


def split(x):
    first = x.astype(BF16)
    return jnp.concatenate([first, (x - first.astype(F32)).astype(BF16)], axis=1)


def folded(x):
    half = x.shape[1] // 2
    return x[:, :half] + x[:, half:]


def dot(a, b):
    return lax.dot_general(a, b, (((1,), (0,)), ((), ())), preferred_element_type=F32)


def dot_nt(a, b):
    return lax.dot_general(a, b, (((1,), (1,)), ((), ())), preferred_element_type=F32)


def pixel_side(pixel):
    places = [swap_groups(pixel[8 * half : 8 * half + 8]) for half in range(2)]
    lows = [
        jnp.where((p & 15)[:, None, :] == iota((8, 16, 128), 1), 1.0, 0.0).reshape(128, 128)
        for p in places
    ]
    return jnp.concatenate(places, axis=1), jnp.concatenate(lows, axis=1).astype(BF16)


def block_sums(area, places, lows):
    firsts, seconds = [], []
    for half in range(2):
        a = swap_groups(area[8 * half : 8 * half + 8])
        high = places[:, 128 * half : 128 * half + 128] >> 4
        a1 = a.astype(BF16).astype(F32)
        a2 = a - a1
        is_high = high[:, None, :] == iota((8, 8, 128), 1)
        firsts.append(jnp.where(is_high, a1[:, None, :], 0.0).reshape(64, 128))
        seconds.append(jnp.where(is_high, a2[:, None, :], 0.0).reshape(64, 128))
    left = jnp.concatenate(
        [jnp.concatenate(firsts, axis=1), jnp.concatenate(seconds, axis=1)], axis=0
    ).astype(BF16)
    out = dot_nt(left, lows)
    out = out[:64] + out[64:]
    group = iota((8, 128), 1) >> 4
    own = out[0:8]
    for b in range(1, 8):
        own = jnp.where(group == b, out[8 * b : 8 * b + 8], own)
    return swap_groups(own)


STEP = (0, 2, -2, 1, 3, -1, -3, 4)
SPANS = ((3, 5, 1), (5, 7, -1), (7, 8, 2), (0, 3, 0))
TABLES = ((1, 4, 7), (2, 6, 7), (0, 3, 5))


def exchange(
    nr, nz, cap,
    elev, lay, pix, target_in, local_in, back_in,
    gamma, found, places,
    target, local, back, low_table, epad, layv, pixv, look, put_low, put_high, pick, oht, oh, hist,
    edge_out, edge_in, sendb, recvb, idsend, idrecv, named, partial, cin, packed, gin, backb, retb,
    in_sem, halo_send, halo_recv, id_send, id_recv, name_send, name_recv, out_send, out_recv,
    sum_send, sum_recv, gam_send, gam_recv, ret_send, ret_recv,
):
    rows, cols = elev.shape
    tb = target_in.shape[1]
    dests = nr * nz
    hc = cap // 2
    n4 = nr * hc
    tiles = cols // 128
    r, c, s = lax.axis_index("maprow"), lax.axis_index("mapcol"), lax.axis_index("sect")

    def plane(step):
        return lax.rem(c + (step + nz), nz)

    def peer_of(i):
        if nr != 16:
            return lax.rem(r + 1 + i, nr)

        def away(n):
            return jnp.where(n == 0, 2, jnp.where(n == 3, 0, 2 * n - 1))

        return (r // 4 + away(i // 4)) % 4 * 4 + (r % 4 + away(i % 4)) % 4

    west = {"mapcol": lax.rem(c + nz - 1 + s, nz), "sect": 1 - s}
    east = {"mapcol": lax.rem(c + s, nz), "sect": 1 - s}
    north, south = {"maprow": lax.rem(r + nr - 1, nr)}, {"maprow": lax.rem(r + 1, nr)}

    barrier = pltpu.get_barrier_semaphore()

    def greet(j, carry):
        peer = peer_of(j)
        for step in (2, -2, 1, -1):
            pl.semaphore_signal(
                barrier, inc=1, device_id={"maprow": peer, "mapcol": plane(step)},
                device_id_type=MESH,
            )
        return carry

    def greet_plane(j, carry):
        pl.semaphore_signal(
            barrier, inc=1, device_id={"maprow": peer_of(j)}, device_id_type=MESH
        )
        return carry

    for neighbour in (west, east):
        pl.semaphore_signal(barrier, inc=1, device_id=neighbour, device_id_type=MESH)
    lax.fori_loop(0, nr, greet, 0)
    lax.fori_loop(0, nr - 1, greet_plane, 0)

    loads = [
        pltpu.make_async_copy(target_in, target, in_sem.at[0]),
        pltpu.make_async_copy(local_in, local, in_sem.at[1]),
        pltpu.make_async_copy(pix, pixv, in_sem.at[2]),
        pltpu.make_async_copy(elev, epad.at[8 : 8 + rows, 128 : 128 + cols], in_sem.at[3]),
        pltpu.make_async_copy(lay, layv, in_sem.at[4]),
        pltpu.make_async_copy(back_in, back, in_sem.at[5]),
    ]
    for load in loads:
        load.start()

    loads[0].wait()
    loads[1].wait()
    name = target[...]
    ahead = ((name & (nz - 1)) + (nz - c)) & (nz - 1)
    order = jnp.zeros((1, tb), jnp.int32)
    for p, step in enumerate(STEP):
        order = jnp.where(ahead == step % nz, p, order)
    spot = (name >> (nz.bit_length() - 1)) * nz + order
    onehot = iota((dests, tb), 0) == spot
    earlier = jnp.where(iota((tb, tb), 0) < iota((tb, tb), 1), 1.0, 0.0).astype(BF16)
    running = dot(jnp.where(onehot, 1.0, 0.0).astype(BF16), earlier)
    rank = jnp.sum(jnp.where(onehot, running, 0.0), axis=0, keepdims=True)
    slot = (spot * cap).astype(F32) + rank
    ids = jnp.where(onehot, local[...].astype(F32), 0.0).astype(BF16)
    high = rank >= float(hc)
    within = jnp.where(high, rank - float(hc), rank)
    at_lane = (r * hc).astype(F32) + within + jnp.where(high, float(n4), 0.0)
    lanes = jnp.where(iotaf((128, tb), 0) == at_lane, 1.0, 0.0).astype(BF16)
    idsend[...] = dot_nt(ids, lanes).reshape(nr, nz, 128)
    idrecv[pl.ds(r, 1)] = idsend[pl.ds(r, 1)]

    loads[2].wait()
    group_bands = 8 if rows % (8 * BR) == 0 else 2

    def pixels(i, carry):
        for n in range(group_bands):
            top = pl.multiple_of(i * (group_bands * BR) + n * BR, BR)
            for j in range(tiles):
                unit = i * (group_bands * tiles) + n * tiles + j
                place, low = pixel_side(pixv[pl.ds(top, BR), 128 * j : 128 * j + 128])
                places[pl.ds(pl.multiple_of(8 * unit, 8), 8), :] = place
                low_table[unit] = low
        return carry

    lax.fori_loop(0, rows // (group_bands * BR), pixels, 0)

    loads[3].wait()
    edge_out[0] = jnp.transpose(epad[8 : 8 + rows, 128:256])[0:8]
    edge_out[1] = jnp.transpose(epad[8 : 8 + rows, cols : 128 + cols])[120:128]

    pl.semaphore_wait(barrier, 5 * nr - 1 + 2)

    inner = slice(128, 128 + cols)
    halos = [
        (epad.at[rows : rows + 8, inner], epad.at[0:8, inner], south),
        (epad.at[8:16, inner], epad.at[rows + 8 : rows + 16, inner], north),
        (edge_out.at[0], edge_in.at[0], west),
        (edge_out.at[1], edge_in.at[1], east),
    ]
    halos = [
        pltpu.make_async_remote_copy(
            src_ref=src, dst_ref=dst, send_sem=halo_send.at[i], recv_sem=halo_recv.at[i],
            device_id=where, device_id_type=MESH,
        )
        for i, (src, dst, where) in enumerate(halos)
    ]
    for halo in halos:
        halo.start()

    def name_slots(i, carry):
        peer = peer_of(i)
        pltpu.make_async_remote_copy(
            src_ref=idsend.at[peer], dst_ref=idrecv.at[r], send_sem=id_send, recv_sem=id_recv,
            device_id={"maprow": peer}, device_id_type=MESH,
        ).start()
        return carry

    lax.fori_loop(0, nr - 1, name_slots, 0)

    def to_peers(source, sink, send_sem, recv_sem, way):
        def start(span, peer):
            p0, p1, step = span
            where = plane(way * step)
            if step == 2:
                where = jnp.where((r + peer) % 2 == 0, plane(2 * way), plane(-2 * way))
            k = 0 if step == 0 else 1
            pltpu.make_async_remote_copy(
                src_ref=source(p0, p1, peer), dst_ref=sink(p0, p1, r),
                send_sem=send_sem.at[k], recv_sem=recv_sem.at[k],
                device_id={"maprow": peer, "mapcol": where}, device_id_type=MESH,
            ).start()

        def far(j, carry):
            for span in SPANS[:3]:
                start(span, peer_of(j))
            return carry

        def near(j, carry):
            start(SPANS[3], peer_of(j))
            return carry

        lax.fori_loop(0, nr, far, 0)
        lax.fori_loop(0, nr - 1, near, 0)

    def done(part, sem):
        pltpu.make_async_copy(part, part, sem).wait()

    def done_rows(buffer, sem):
        done(buffer.at[3:nz], sem.at[1])
        done(buffer.at[0:3, 0 : (nr - 1) * hc], sem.at[0])

    def of_rows(buffer):
        return lambda p0, p1, i: buffer.at[p0:p1, pl.ds(i * hc, hc)]

    i0 = iota((nz * n4, 1), 0)
    row_slot = (((i0 % n4) // hc) * (nz * cap) + (i0 // n4) * cap + i0 % hc).astype(F32)
    put_low[...] = jnp.where(row_slot == slot, 1.0, 0.0).astype(BF16)
    put_high[...] = jnp.where(row_slot + float(hc) == slot, 1.0, 0.0).astype(BF16)

    column = ((c * 2 + s) * cols + iota((1, cols), 1)).astype(F32)
    incidence = 0.52 + 0.28 * (column + 0.5) / float(cols * nz * 2)
    sine, heading = jnp.sin(incidence), jnp.full((1, cols), HEADING, F32)
    look[0:1, :] = -sine * jnp.cos(heading) / (2.0 * CELL_SPACING)
    look[1:2, :] = -sine * jnp.sin(heading) / (2.0 * CELL_SPACING)
    look[2:3, :] = jnp.cos(incidence)

    loads[4].wait()

    def unit_sums(i, j):
        lane = iota((BR, 128), 1)
        top = BR * i
        at = slice(128 * j, 128 * j + 128)
        around = epad[top : top + 32, 128 + 128 * j : 256 + 128 * j]
        before, here, after = (
            epad[top + 8 : top + 24, 128 * n : 128 * n + 128] for n in (j, j + 1, j + 2)
        )
        before = pltpu.roll(jnp.where(lane == 127, before, here), 1, 1)
        after = pltpu.roll(jnp.where(lane == 0, after, here), 127, 1)
        rise_cols = after - before
        rise_rows = around[9:25] - around[7:23]
        facing = look[2:3, at] - rise_cols * look[0:1, at] - rise_rows * look[1:2, at]
        lit = (1 - layv[top : top + BR, at]).astype(F32)
        unit = i * tiles + j
        span = slice(8 * unit, 8 * unit + 8)
        area = jnp.maximum(facing, 0.0) * lit
        hist[span, :] = block_sums(area, places[span, :], low_table[unit])

    nb = rows // BR
    inside = [(i, j) for i in range(1, nb - 1) for j in range(1, tiles - 1)]
    for i, j in inside:
        unit_sums(i, j)

    for halo in halos:
        halo.wait_recv()

    @pl.when(r == 0)
    def _():
        epad[0:8, inner] = jnp.zeros((8, cols), F32)

    @pl.when(r == nr - 1)
    def _():
        epad[rows + 8 : rows + 16, inner] = jnp.zeros((8, cols), F32)

    first, last = (c == 0) & (s == 0), (c == nz - 1) & (s == 1)
    west_edge = jnp.where(first, 0.0, edge_in[1, 7:8, :])
    east_edge = jnp.where(last, 0.0, edge_in[0, 0:1, :])
    epad[8 : 8 + rows, 0:128] = jnp.transpose(jnp.broadcast_to(west_edge, (128, rows)))
    epad[8 : 8 + rows, 128 + cols : 256 + cols] = jnp.transpose(
        jnp.broadcast_to(east_edge, (128, rows))
    )
    for i in range(nb):
        for j in range(tiles):
            if (i, j) not in inside:
                unit_sums(i, j)

    done(idrecv.at[0 : nr - 1], id_recv)
    names = idrecv[0]
    for i in range(1, nr):
        names = names + idrecv[i]
    named[0] = names
    tells = [
        pltpu.make_async_remote_copy(
            src_ref=named.at[0], dst_ref=named.at[n + 1],
            send_sem=name_send.at[n], recv_sem=name_recv.at[n],
            device_id={"mapcol": plane(step)}, device_id_type=MESH,
        )
        for n, step in enumerate((1, -1, 2, -2))
    ]
    for tell in tells:
        tell.start()

    left = iota((nz * n4, 128), 1) < 64
    sums = hist[...]
    lower = folded(dot(put_low[...], split(sums)))
    upper = folded(dot(put_high[...], split(pltpu.roll(sums, 64, 1))))
    sendb[0] = jnp.where(left, lower, upper).reshape(nz, n4, 128)
    sendb[1] = jnp.where(left, upper, lower).reshape(nz, n4, 128)
    mine = pl.ds(r * hc, hc)
    for q in range(2):
        recvb[q, 0:3, mine] = sendb[q, 0:3, mine]
        to_peers(of_rows(sendb.at[q]), of_rows(recvb.at[q]), out_send.at[q], out_recv.at[q], 1)

    row_of = (
        within
        + (((spot & (nz - 1)) * nr + (spot >> (nz.bit_length() - 1))) * hc).astype(F32)
        + jnp.where(high, float(nz * n4), 0.0)
    )
    row_down = jnp.transpose(jnp.broadcast_to(row_of, (128, tb)))
    high_down = row_down >= float(nz * n4)
    row_down = jnp.where(high_down, row_down - float(nz * n4), row_down)
    for n in range(0, nz * n4, 128):
        width = min(128, nz * n4 - n)
        pick[:, n : n + width] = jnp.where(
            row_down[:, :width] == iotaf((1, width), 1) + float(n), 1.0, 0.0
        ).astype(BF16)

    loads[5].wait()
    for tell in tells:
        tell.wait_recv()
    from_step = (0, 0, 0, 1, 1, 2, 2)
    lane = iota((1, 128), 1)
    even = ((lane % n4) // hc + r) % 2 == 0
    for t, table in enumerate(TABLES):
        for m, p in enumerate(table):
            name = named[from_step[p] if p < 7 else 3 + t, p : p + 1, :]
            if p == 7:
                name = jnp.where(even == (t == 0), name, -1.0)
            if 2 * n4 < 128:
                name = jnp.where(lane < 2 * n4, name, -1.0)
            wide = jnp.broadcast_to(name, (128, 128))
            at = slice(128 * m, 128 * m + 128)
            oht[t, :, at] = jnp.where(wide == iotaf((128, 128), 0), 1.0, 0.0).astype(BF16)
            oh[t, at, :] = jnp.where(
                jnp.transpose(wide) == iotaf((128, 128), 1), 1.0, 0.0
            ).astype(BF16)
    half = iota((64, 128), 1) < 64
    backs = [back[0:64, :], back[64:128, :]]
    backs = [
        jnp.where(half, backs[0], pltpu.roll(backs[1], 64, 1)),
        jnp.where(half, pltpu.roll(backs[0], 64, 1), backs[1]),
    ]

    def filled(x):
        if 2 * n4 == 128:
            return x
        return jnp.concatenate([x, jnp.zeros((128 - 2 * n4, 128), F32)], axis=0)

    def table_of(q, t):
        given = []
        for p in TABLES[t]:
            x = recvb[q, p]
            y = pltpu.roll(x, 64, 1)
            given.append(split(filled(jnp.concatenate([x, y] if q == 0 else [y, x], axis=0))))
        total = folded(dot(oht[t], jnp.concatenate(given, axis=0)))
        return jnp.where(half, total[0:64], pltpu.roll(total[64:128], 64, 1))

    def two_steps(source, sink, send_sem, recv_sem, way):
        return pltpu.make_async_remote_copy(
            src_ref=source, dst_ref=sink.at[way],
            send_sem=send_sem.at[way], recv_sem=recv_sem.at[way],
            device_id={"mapcol": plane((2, -2)[way])}, device_id_type=MESH,
        )

    hops = []
    own = []
    for q in range(2):
        done_rows(recvb.at[q], out_recv.at[q])
        for way in range(2):
            partial[q, way] = table_of(q, way)
            hops.append(
                two_steps(partial.at[q, way], cin.at[q], sum_send.at[q], sum_recv.at[q], way)
            )
            hops[-1].start()
        own.append(table_of(q, 2))
    gammas = []
    for q in range(2):
        hops[2 * q].wait_recv()
        hops[2 * q + 1].wait_recv()
        total = own[q] + cin[q, 0] + cin[q, 1]
        packed[q] = backs[q] / jnp.maximum(total, 1.0)
        for way in range(2):
            gammas.append(
                two_steps(packed.at[q], gin.at[q], gam_send.at[q], gam_recv.at[q], way)
            )
            gammas[-1].start()
    halves = [(packed[q], pltpu.roll(packed[q], 64, 1)) for q in range(2)]
    gamma[0:64] = jnp.where(half, halves[0][0], halves[1][1])
    gamma[64:128] = jnp.where(half, halves[0][1], halves[1][0])

    def served(q, t):
        x = packed[q] if t == 2 else gin[q, 1 - t]
        y = pltpu.roll(x, 64, 1)
        whole = jnp.concatenate([jnp.where(half, x, y), jnp.where(half, y, x)], axis=0)
        asked = folded(dot(oh[t], split(whole)))
        slots = iota((n4, 128), 1) < 64
        return [
            jnp.where(
                slots, asked[128 * m : 128 * m + n4], asked[128 * m + n4 : 128 * m + 2 * n4]
            )
            for m in range(3)
        ]

    for q in range(2):
        for p, x in zip(TABLES[2], served(q, 2)):
            backb[q, p] = x
        gammas[2 * q].wait_recv()
        gammas[2 * q + 1].wait_recv()
        ahead_rows, behind_rows = served(q, 0), served(q, 1)
        backb[q, 1], backb[q, 4] = ahead_rows[0], ahead_rows[1]
        backb[q, 2], backb[q, 6] = behind_rows[0], behind_rows[1]
        backb[q, 7] = ahead_rows[2] + behind_rows[2]
        retb[q, 0:3, mine] = backb[q, 0:3, mine]
        to_peers(of_rows(backb.at[q]), of_rows(retb.at[q]), ret_send.at[q], ret_recv.at[q], -1)

    left = iota((tb, 128), 1) < 64
    for q in range(2):
        done_rows(retb.at[q], ret_recv.at[q])
        x = folded(dot(pick[...], split(retb[q].reshape(nz * n4, 128))))
        y = pltpu.roll(x, 64, 1)
        if q == 0:
            found[...] = jnp.where(high_down, y, x)
        else:
            found[...] = jnp.where(left, found[...], jnp.where(high_down, x, y))

    for halo in halos:
        halo.wait_send()
    done(idsend.at[0 : nr - 1], id_send)
    for tell in tells:
        tell.wait_send()
    for q in range(2):
        done_rows(sendb.at[q], out_send.at[q])
        done_rows(backb.at[q], ret_send.at[q])
    for one in (*hops, *gammas):
        one.wait_send()


def lookup(found, places, gamma, gamma_out, out, cells, sems):
    rows, cols = out.shape
    tiles = cols // 128
    chunk = 64 if rows % 64 == 0 else rows
    copies = [pltpu.make_async_copy(gamma, gamma_out, sems.at[0])]
    copies[0].start()
    for unit in range(rows // BR * tiles):
        span = slice(8 * unit, 8 * unit + 8)
        for half in range(2):
            place = places[span, 128 * half : 128 * half + 128]
            top, at = BR * (unit // tiles) + 8 * half, 128 * (unit % tiles)
            cells[top : top + 8, at : at + 128] = jnp.take_along_axis(
                found[span, :], place, axis=1
            )
    for k in range(rows // chunk):
        for top in range(k * chunk, (k + 1) * chunk, 8):
            for at in range(0, cols, 128):
                piece = (slice(top, top + 8), slice(at, at + 128))
                cells[piece] = swap_groups(cells[piece])
        part = slice(k * chunk, (k + 1) * chunk)
        copies.append(pltpu.make_async_copy(cells.at[part], out.at[part], sems.at[k + 1]))
        copies[-1].start()
    for copy in copies:
        copy.wait()


def per_device(nr, nz, elevation, layover, footprint_pixel, footprint_device, local_block, backscatter):
    rows, cols = elevation.shape
    tb = local_block.shape[1]
    cap = max(2, 2 * tb // (nr * nz))
    n4 = nr * cap // 2
    held = backscatter.shape[0]
    vmem = pl.BlockSpec(memory_space=pltpu.VMEM)
    hbm = pl.BlockSpec(memory_space=pltpu.HBM)
    dma = pltpu.SemaphoreType.DMA
    gamma, found, places = pl.pallas_call(
        functools.partial(exchange, nr, nz, cap),
        out_shape=(
            jax.ShapeDtypeStruct((held, PIX), F32),
            jax.ShapeDtypeStruct((tb, PIX), F32),
            jax.ShapeDtypeStruct((tb, BR * BC), jnp.int32),
        ),
        in_specs=[hbm] * 6,
        out_specs=(vmem, vmem, vmem),
        scratch_shapes=[
            pltpu.VMEM((1, tb), jnp.int32),
            pltpu.VMEM((1, tb), jnp.int32),
            pltpu.VMEM((held, PIX), F32),
            pltpu.VMEM((tb // 8, 128, BR * BC), BF16),
            pltpu.VMEM((rows + 16, cols + 256), F32),
            pltpu.VMEM((rows, cols), jnp.int32),
            pltpu.VMEM((rows, cols), jnp.int32),
            pltpu.VMEM((8, cols), F32),
            pltpu.VMEM((nz * n4, tb), BF16),
            pltpu.VMEM((nz * n4, tb), BF16),
            pltpu.VMEM((tb, nz * n4), BF16),
            pltpu.VMEM((3, 128, 3 * 128), BF16),
            pltpu.VMEM((3, 3 * 128, 128), BF16),
            pltpu.VMEM((tb, PIX), F32),
            pltpu.VMEM((2, 8, rows), F32),
            pltpu.VMEM((2, 8, rows), F32),
            pltpu.VMEM((2, nz, n4, 128), F32),
            pltpu.VMEM((2, nz, n4, 128), F32),
            pltpu.VMEM((nr, nz, 128), F32),
            pltpu.VMEM((nr, nz, 128), F32),
            pltpu.VMEM((5, nz, 128), F32),
            pltpu.VMEM((2, 2, 64, 128), F32),
            pltpu.VMEM((2, 2, 64, 128), F32),
            pltpu.VMEM((2, 64, 128), F32),
            pltpu.VMEM((2, 2, 64, 128), F32),
            pltpu.VMEM((2, nz, n4, 128), F32),
            pltpu.VMEM((2, nz, n4, 128), F32),
            dma((6,)),
            dma((4,)),
            dma((4,)),
            dma,
            dma,
            dma((4,)),
            dma((4,)),
            *([dma((2, 2))] * 8),
        ],
        compiler_params=pltpu.CompilerParams(
            collective_id=0, has_side_effects=True, vmem_limit_bytes=40 * 2**20
        ),
    )(
        *(
            pltpu.with_memory_space_constraint(x, pltpu.HBM)
            for x in (
                elevation, layover, footprint_pixel,
                footprint_device.reshape(1, tb), local_block, backscatter,
            )
        )
    )
    return pl.pallas_call(
        lookup,
        out_shape=(
            jax.ShapeDtypeStruct((held, PIX), F32),
            jax.ShapeDtypeStruct((rows, cols), F32),
        ),
        in_specs=[vmem, vmem, vmem],
        out_specs=(hbm, hbm),
        scratch_shapes=[pltpu.VMEM((rows, cols), F32), dma((1 + max(1, rows // 64),))],
        compiler_params=pltpu.CompilerParams(vmem_limit_bytes=8 * 2**20),
    )(found, places, gamma)


def solution(mesh):
    in_specs = (
        P("maprow", ("mapcol", "sect")),
        P("maprow", ("mapcol", "sect")),
        P("maprow", ("mapcol", "sect")),
        P(("maprow", "mapcol", "sect"), None, None),
        P(("maprow", "mapcol", "sect"), None),
        P(("maprow", "mapcol", "sect"), None),
    )
    out_specs = (P(("maprow", "mapcol", "sect"), None), P("maprow", ("mapcol", "sect")))
    return jax.shard_map(
        functools.partial(per_device, mesh.shape["maprow"], mesh.shape["mapcol"]),
        mesh=mesh,
        in_specs=in_specs,
        out_specs=out_specs,
        check_vma=False,
    )
```

```python
import functools

import jax
import jax.numpy as jnp
from jax import lax
from jax.experimental import pallas as pl
from jax.experimental.pallas import tpu as pltpu
from jax.sharding import PartitionSpec as P

BR = 16
BC = 16
PIX = 128
CELL_SPACING = 10.0
HEADING = 0.2
MESH = pl.DeviceIdType.MESH
F32 = jnp.float32
BF16 = jnp.bfloat16


def iota(shape, dim):
    return lax.broadcasted_iota(jnp.int32, shape, dim)


def iotaf(shape, dim):
    return iota(shape, dim).astype(F32)


def swap_groups(x):
    lane, row = iota((8, 128), 1), iota((8, 128), 0)
    x = pltpu.roll(x, 0, 1, stride=16, stride_axis=0)
    x = jnp.take_along_axis(x, ((lane >> 4) - row) & 7, axis=0)
    return jnp.take_along_axis(x, (lane + 16 * row) & 127, axis=1)


def split(x):
    first = x.astype(BF16)
    return jnp.concatenate([first, (x - first.astype(F32)).astype(BF16)], axis=1)


def folded(x):
    half = x.shape[1] // 2
    return x[:, :half] + x[:, half:]


def dot(a, b):
    return lax.dot_general(a, b, (((1,), (0,)), ((), ())), preferred_element_type=F32)


def dot_nt(a, b):
    return lax.dot_general(a, b, (((1,), (1,)), ((), ())), preferred_element_type=F32)


def pixel_side(pixel):
    places = [swap_groups(pixel[8 * half : 8 * half + 8]) for half in range(2)]
    lows = [
        jnp.where((p & 15)[:, None, :] == iota((8, 16, 128), 1), 1.0, 0.0).reshape(128, 128)
        for p in places
    ]
    return jnp.concatenate(places, axis=1), jnp.concatenate(lows, axis=1).astype(BF16)


def block_sums(area, places, lows):
    firsts, seconds = [], []
    for half in range(2):
        a = swap_groups(area[8 * half : 8 * half + 8])
        high = places[:, 128 * half : 128 * half + 128] >> 4
        a1 = a.astype(BF16).astype(F32)
        a2 = a - a1
        is_high = high[:, None, :] == iota((8, 8, 128), 1)
        firsts.append(jnp.where(is_high, a1[:, None, :], 0.0).reshape(64, 128))
        seconds.append(jnp.where(is_high, a2[:, None, :], 0.0).reshape(64, 128))
    left = jnp.concatenate(
        [jnp.concatenate(firsts, axis=1), jnp.concatenate(seconds, axis=1)], axis=0
    ).astype(BF16)
    out = dot_nt(left, lows)
    out = out[:64] + out[64:]
    group = iota((8, 128), 1) >> 4
    own = out[0:8]
    for b in range(1, 8):
        own = jnp.where(group == b, out[8 * b : 8 * b + 8], own)
    return swap_groups(own)


STEP = (0, 2, -2, 1, 3, -1, -3, 4)
SPANS = ((7, 8, 2), (3, 5, 1), (5, 7, -1), (0, 3, 0))
AWAY = (
    (2, 2), (1, 3), (3, 1), (2, 1), (1, 2), (3, 3), (1, 1), (2, 3),
    (3, 2), (2, 0), (0, 2), (1, 0), (3, 0), (0, 1), (0, 3), (0, 0),
)
TABLES = ((1, 4, 7), (2, 6, 7), (0, 3, 5))


def exchange(
    nr, nz, cap,
    elev, lay, pix, target_in, local_in, back_in,
    gamma, found, places,
    target, local, back, low_table, epad, layv, pixv, look, put_low, put_high, pick, oht, oh, hist,
    edge_out, edge_in, sendb, recvb, idsend, idrecv, named, partial, cin, packed, gin, backb, retb,
    plane_sem, steps_sem, in_sem, halo_send, halo_recv, id_send, id_recv, name_send, name_recv, out_send, out_recv,
    sum_send, sum_recv, gam_send, gam_recv, ret_send, ret_recv,
):
    rows, cols = elev.shape
    tb = target_in.shape[1]
    dests = nr * nz
    hc = cap // 2
    n4 = nr * hc
    tiles = cols // 128
    r, c, s = lax.axis_index("maprow"), lax.axis_index("mapcol"), lax.axis_index("sect")

    def plane(step):
        return lax.rem(c + (step + nz), nz)

    if nr == 16:
        along_x = [(r // 4 + n) % 4 * 4 for n in range(4)]
        along_y = [(r % 4 + n) % 4 for n in range(4)]
        peers = [along_x[x] + along_y[y] for x, y in AWAY]
        line_x = [along_x[n] + along_y[0] for n in (2, 1, 3)]
        line_y = [along_x[0] + along_y[n] for n in (2, 1, 3)]
    else:
        peers = [lax.rem(r + 1 + i, nr) for i in range(nr)]
        line_x, line_y = [], peers[:-1]

    west = {"mapcol": lax.rem(c + nz - 1 + s, nz), "sect": 1 - s}
    east = {"mapcol": lax.rem(c + s, nz), "sect": 1 - s}
    north, south = {"maprow": lax.rem(r + nr - 1, nr)}, {"maprow": lax.rem(r + 1, nr)}

    barrier = pltpu.get_barrier_semaphore()

    line_x = [{"maprow": i} for i in line_x]
    line_y = [{"maprow": i} for i in line_y]
    line_z = [{"mapcol": plane(step)} for step in (2, -2, 1, -1)]
    greeted = (north, south, west, east, *line_z, *line_x, *line_y)

    def greet(devices, sem):
        for device in devices:
            pl.semaphore_signal(sem, inc=1, device_id=device, device_id_type=MESH)

    greet(greeted, barrier)

    loads = [
        pltpu.make_async_copy(target_in, target, in_sem.at[0]),
        pltpu.make_async_copy(local_in, local, in_sem.at[1]),
        pltpu.make_async_copy(pix, pixv, in_sem.at[2]),
        pltpu.make_async_copy(elev, epad.at[8 : 8 + rows, 128 : 128 + cols], in_sem.at[3]),
        pltpu.make_async_copy(lay, layv, in_sem.at[4]),
        pltpu.make_async_copy(back_in, back, in_sem.at[5]),
    ]
    for load in loads:
        load.start()

    loads[0].wait()
    loads[1].wait()
    name = target[...]
    ahead = ((name & (nz - 1)) + (nz - c)) & (nz - 1)
    order = jnp.zeros((1, tb), jnp.int32)
    for p, step in enumerate(STEP):
        order = jnp.where(ahead == step % nz, p, order)
    spot = (name >> (nz.bit_length() - 1)) * nz + order
    onehot = iota((dests, tb), 0) == spot
    earlier = jnp.where(iota((tb, tb), 0) < iota((tb, tb), 1), 1.0, 0.0).astype(BF16)
    running = dot(jnp.where(onehot, 1.0, 0.0).astype(BF16), earlier)
    rank = jnp.sum(jnp.where(onehot, running, 0.0), axis=0, keepdims=True)
    slot = (spot * cap).astype(F32) + rank
    ids = jnp.where(onehot, local[...].astype(F32), 0.0).astype(BF16)
    high = rank >= float(hc)
    within = jnp.where(high, rank - float(hc), rank)
    at_lane = (r * hc).astype(F32) + within + jnp.where(high, float(n4), 0.0)
    lanes = jnp.where(iotaf((128, tb), 0) == at_lane, 1.0, 0.0).astype(BF16)
    idsend[...] = dot_nt(ids, lanes).reshape(nr, nz, 128)
    idrecv[pl.ds(r, 1)] = idsend[pl.ds(r, 1)]

    loads[3].wait()
    edge_out[0] = jnp.transpose(epad[8 : 8 + rows, 128:256])[0:8]
    edge_out[1] = jnp.transpose(epad[8 : 8 + rows, cols : 128 + cols])[120:128]

    pl.semaphore_wait(barrier, len(greeted))

    inner = slice(128, 128 + cols)
    halos = [
        (epad.at[rows : rows + 8, inner], epad.at[0:8, inner], south),
        (epad.at[8:16, inner], epad.at[rows + 8 : rows + 16, inner], north),
        (edge_out.at[0], edge_in.at[0], west),
        (edge_out.at[1], edge_in.at[1], east),
    ]
    halos = [
        pltpu.make_async_remote_copy(
            src_ref=src, dst_ref=dst, send_sem=halo_send.at[i], recv_sem=halo_recv.at[i],
            device_id=where, device_id_type=MESH,
        )
        for i, (src, dst, where) in enumerate(halos)
    ]
    for halo in halos:
        halo.start()
    greet(line_x, plane_sem)

    loads[2].wait()
    group_bands = 8 if rows % (8 * BR) == 0 else 2

    def pixels(i, carry):
        for n in range(group_bands):
            top = pl.multiple_of(i * (group_bands * BR) + n * BR, BR)
            for j in range(tiles):
                unit = i * (group_bands * tiles) + n * tiles + j
                place, low = pixel_side(pixv[pl.ds(top, BR), 128 * j : 128 * j + 128])
                places[pl.ds(pl.multiple_of(8 * unit, 8), 8), :] = place
                low_table[unit] = low
        return carry

    lax.fori_loop(0, rows // (group_bands * BR), pixels, 0)

    if line_x:
        pl.semaphore_wait(plane_sem, len(line_x))
    greet(line_z, steps_sem)

    for peer in peers[:-1]:
        pltpu.make_async_remote_copy(
            src_ref=idsend.at[peer], dst_ref=idrecv.at[r], send_sem=id_send, recv_sem=id_recv,
            device_id={"maprow": peer}, device_id_type=MESH,
        ).start()

    def to_peers(source, sink, send_sem, recv_sem, way):
        def start(span, peer):
            p0, p1, step = span
            where = plane(way * step)
            if step == 2:
                where = jnp.where((r + peer) % 2 == 0, plane(2 * way), plane(-2 * way))
            k = 0 if step == 0 else 1
            pltpu.make_async_remote_copy(
                src_ref=source(p0, p1, peer), dst_ref=sink(p0, p1, r),
                send_sem=send_sem.at[k], recv_sem=recv_sem.at[k],
                device_id={"maprow": peer, "mapcol": where}, device_id_type=MESH,
            ).start()

        for i, peer in enumerate(peers):
            for span in SPANS:
                if i < nr - 1 or span[2] != 0:
                    start(span, peer)

    def done(part, sem):
        pltpu.make_async_copy(part, part, sem).wait()

    def done_rows(buffer, sem):
        done(buffer.at[3:nz], sem.at[1])
        done(buffer.at[0:3, 0 : (nr - 1) * hc], sem.at[0])

    def of_rows(buffer):
        return lambda p0, p1, i: buffer.at[p0:p1, pl.ds(i * hc, hc)]

    i0 = iota((nz * n4, 1), 0)
    row_slot = (((i0 % n4) // hc) * (nz * cap) + (i0 // n4) * cap + i0 % hc).astype(F32)
    put_low[...] = jnp.where(row_slot == slot, 1.0, 0.0).astype(BF16)
    put_high[...] = jnp.where(row_slot + float(hc) == slot, 1.0, 0.0).astype(BF16)

    column = ((c * 2 + s) * cols + iota((1, cols), 1)).astype(F32)
    incidence = 0.52 + 0.28 * (column + 0.5) / float(cols * nz * 2)
    sine, heading = jnp.sin(incidence), jnp.full((1, cols), HEADING, F32)
    look[0:1, :] = -sine * jnp.cos(heading) / (2.0 * CELL_SPACING)
    look[1:2, :] = -sine * jnp.sin(heading) / (2.0 * CELL_SPACING)
    look[2:3, :] = jnp.cos(incidence)

    loads[4].wait()

    def unit_sums(i, j):
        lane = iota((BR, 128), 1)
        top = BR * i
        at = slice(128 * j, 128 * j + 128)
        around = epad[top : top + 32, 128 + 128 * j : 256 + 128 * j]
        before, here, after = (
            epad[top + 8 : top + 24, 128 * n : 128 * n + 128] for n in (j, j + 1, j + 2)
        )
        before = pltpu.roll(jnp.where(lane == 127, before, here), 1, 1)
        after = pltpu.roll(jnp.where(lane == 0, after, here), 127, 1)
        rise_cols = after - before
        rise_rows = around[9:25] - around[7:23]
        facing = look[2:3, at] - rise_cols * look[0:1, at] - rise_rows * look[1:2, at]
        lit = (1 - layv[top : top + BR, at]).astype(F32)
        unit = i * tiles + j
        span = slice(8 * unit, 8 * unit + 8)
        area = jnp.maximum(facing, 0.0) * lit
        hist[span, :] = block_sums(area, places[span, :], low_table[unit])

    nb = rows // BR
    inside = [(i, j) for i in range(1, nb - 1) for j in range(1, tiles - 1)]
    for i, j in inside:
        unit_sums(i, j)

    for halo in halos:
        halo.wait_recv()

    @pl.when(r == 0)
    def _():
        epad[0:8, inner] = jnp.zeros((8, cols), F32)

    @pl.when(r == nr - 1)
    def _():
        epad[rows + 8 : rows + 16, inner] = jnp.zeros((8, cols), F32)

    first, last = (c == 0) & (s == 0), (c == nz - 1) & (s == 1)
    west_edge = jnp.where(first, 0.0, edge_in[1, 7:8, :])
    east_edge = jnp.where(last, 0.0, edge_in[0, 0:1, :])
    epad[8 : 8 + rows, 0:128] = jnp.transpose(jnp.broadcast_to(west_edge, (128, rows)))
    epad[8 : 8 + rows, 128 + cols : 256 + cols] = jnp.transpose(
        jnp.broadcast_to(east_edge, (128, rows))
    )
    for i in range(nb):
        for j in range(tiles):
            if (i, j) not in inside:
                unit_sums(i, j)

    pl.semaphore_wait(steps_sem, len(line_z))

    left = iota((nz * n4, 128), 1) < 64
    sums = hist[...]
    lower = folded(dot(put_low[...], split(sums)))
    upper = folded(dot(put_high[...], split(pltpu.roll(sums, 64, 1))))
    sendb[0] = jnp.where(left, lower, upper).reshape(nz, n4, 128)
    sendb[1] = jnp.where(left, upper, lower).reshape(nz, n4, 128)
    mine = pl.ds(r * hc, hc)
    for q in range(2):
        recvb[q, 0:3, mine] = sendb[q, 0:3, mine]
        to_peers(of_rows(sendb.at[q]), of_rows(recvb.at[q]), out_send.at[q], out_recv.at[q], 1)
        if q == 1:
            break

        done(idrecv.at[0 : nr - 1], id_recv)
        names = idrecv[0]
        for i in range(1, nr):
            names = names + idrecv[i]
        named[0] = names
        tells = [
            pltpu.make_async_remote_copy(
                src_ref=named.at[0], dst_ref=named.at[n + 1],
                send_sem=name_send.at[n], recv_sem=name_recv.at[n],
                device_id={"mapcol": plane(step)}, device_id_type=MESH,
            )
            for n, step in enumerate((1, -1, 2, -2))
        ]
        for tell in tells:
            tell.start()

    row_of = (
        within
        + (((spot & (nz - 1)) * nr + (spot >> (nz.bit_length() - 1))) * hc).astype(F32)
        + jnp.where(high, float(nz * n4), 0.0)
    )
    row_down = jnp.transpose(jnp.broadcast_to(row_of, (128, tb)))
    high_down = row_down >= float(nz * n4)
    row_down = jnp.where(high_down, row_down - float(nz * n4), row_down)
    for n in range(0, nz * n4, 128):
        width = min(128, nz * n4 - n)
        pick[:, n : n + width] = jnp.where(
            row_down[:, :width] == iotaf((1, width), 1) + float(n), 1.0, 0.0
        ).astype(BF16)

    loads[5].wait()
    for tell in tells:
        tell.wait_recv()
    from_step = (0, 0, 0, 1, 1, 2, 2)
    lane = iota((1, 128), 1)
    even = ((lane % n4) // hc + r) % 2 == 0
    for t, table in enumerate(TABLES):
        asked = []
        for m, p in enumerate(table):
            name = named[from_step[p] if p < 7 else 3 + t, p : p + 1, :]
            if p == 7:
                name = jnp.where(even == (t == 0), name, -1.0)
            asked.append(name)
            if 2 * n4 < 128:
                name = jnp.where(lane < 2 * n4, name, -1.0)
            wide = jnp.broadcast_to(name, (128, 128))
            at = slice(128 * m, 128 * m + 128)
            oh[t, at, :] = jnp.where(
                jnp.transpose(wide) == iotaf((128, 128), 1), 1.0, 0.0
            ).astype(BF16)
        for half_at in range(2):
            name = jnp.concatenate([x[:, n4 * half_at : n4 * half_at + n4] for x in asked], axis=1)
            oht[t, 128 * half_at : 128 * half_at + 128, :] = jnp.where(
                iotaf((128, 3 * n4), 0) == name, 1.0, 0.0
            ).astype(BF16)
    half = iota((64, 128), 1) < 64
    backs = [back[0:64, :], back[64:128, :]]
    backs = [
        jnp.where(half, backs[0], pltpu.roll(backs[1], 64, 1)),
        jnp.where(half, pltpu.roll(backs[0], 64, 1), backs[1]),
    ]

    whole_half = iota((128, 128), 1) < 64

    def table_of(q, t):
        given = jnp.concatenate([split(recvb[q, p]) for p in TABLES[t]], axis=0)
        both = folded(dot(oht[t], given))
        low, high = both[0:128], both[128:256]
        total = jnp.where(whole_half, low, high) if q == 0 else jnp.where(whole_half, high, low)
        total = total + pltpu.roll(total, 64, 1)
        return jnp.where(half, total[0:64], total[64:128])

    def two_steps(source, sink, send_sem, recv_sem, way):
        return pltpu.make_async_remote_copy(
            src_ref=source, dst_ref=sink.at[way],
            send_sem=send_sem.at[way], recv_sem=recv_sem.at[way],
            device_id={"mapcol": plane((2, -2)[way])}, device_id_type=MESH,
        )

    hops = []
    own = []
    for q in range(2):
        done_rows(recvb.at[q], out_recv.at[q])
        for way in range(2):
            partial[q, way] = table_of(q, way)
            hops.append(
                two_steps(partial.at[q, way], cin.at[q], sum_send.at[q], sum_recv.at[q], way)
            )
            hops[-1].start()
        own.append(table_of(q, 2))
    gammas = []
    for q in range(2):
        hops[2 * q].wait_recv()
        hops[2 * q + 1].wait_recv()
        total = own[q] + cin[q, 0] + cin[q, 1]
        packed[q] = backs[q] / jnp.maximum(total, 1.0)
        for way in range(2):
            gammas.append(
                two_steps(packed.at[q], gin.at[q], gam_send.at[q], gam_recv.at[q], way)
            )
            gammas[-1].start()
    halves = [(packed[q], pltpu.roll(packed[q], 64, 1)) for q in range(2)]
    gamma[0:64] = jnp.where(half, halves[0][0], halves[1][1])
    gamma[64:128] = jnp.where(half, halves[0][1], halves[1][0])

    def served(q, t):
        x = packed[q] if t == 2 else gin[q, 1 - t]
        y = pltpu.roll(x, 64, 1)
        whole = jnp.concatenate([jnp.where(half, x, y), jnp.where(half, y, x)], axis=0)
        asked = folded(dot(oh[t], split(whole)))
        slots = iota((n4, 128), 1) < 64
        return [
            jnp.where(
                slots, asked[128 * m : 128 * m + n4], asked[128 * m + n4 : 128 * m + 2 * n4]
            )
            for m in range(3)
        ]

    for q in range(2):
        for p, x in zip(TABLES[2], served(q, 2)):
            backb[q, p] = x
        gammas[2 * q].wait_recv()
        gammas[2 * q + 1].wait_recv()
        ahead_rows, behind_rows = served(q, 0), served(q, 1)
        backb[q, 1], backb[q, 4] = ahead_rows[0], ahead_rows[1]
        backb[q, 2], backb[q, 6] = behind_rows[0], behind_rows[1]
        backb[q, 7] = ahead_rows[2] + behind_rows[2]
        retb[q, 0:3, mine] = backb[q, 0:3, mine]
        to_peers(of_rows(backb.at[q]), of_rows(retb.at[q]), ret_send.at[q], ret_recv.at[q], -1)

    left = iota((tb, 128), 1) < 64
    for q in range(2):
        done_rows(retb.at[q], ret_recv.at[q])
        x = folded(dot(pick[...], split(retb[q].reshape(nz * n4, 128))))
        y = pltpu.roll(x, 64, 1)
        if q == 0:
            found[...] = jnp.where(high_down, y, x)
        else:
            found[...] = jnp.where(left, found[...], jnp.where(high_down, x, y))

    for halo in halos:
        halo.wait_send()
    done(idsend.at[0 : nr - 1], id_send)
    for tell in tells:
        tell.wait_send()
    for q in range(2):
        done_rows(sendb.at[q], out_send.at[q])
        done_rows(backb.at[q], ret_send.at[q])
    for one in (*hops, *gammas):
        one.wait_send()


def lookup(found, places, gamma, gamma_out, out, cells, sems):
    rows, cols = out.shape
    tiles = cols // 128
    chunk = 64 if rows % 64 == 0 else rows
    copies = [pltpu.make_async_copy(gamma, gamma_out, sems.at[0])]
    copies[0].start()
    for k in range(rows // chunk):
        for unit in range(k * (chunk // BR) * tiles, (k + 1) * (chunk // BR) * tiles):
            span = slice(8 * unit, 8 * unit + 8)
            for half in range(2):
                place = places[span, 128 * half : 128 * half + 128]
                top, at = BR * (unit // tiles) + 8 * half, 128 * (unit % tiles)
                cells[top : top + 8, at : at + 128] = jnp.take_along_axis(
                    found[span, :], place, axis=1
                )
        for top in range(k * chunk, (k + 1) * chunk, 8):
            for at in range(0, cols, 128):
                piece = (slice(top, top + 8), slice(at, at + 128))
                cells[piece] = swap_groups(cells[piece])
        part = slice(k * chunk, (k + 1) * chunk)
        copies.append(pltpu.make_async_copy(cells.at[part], out.at[part], sems.at[k + 1]))
        copies[-1].start()
    for copy in copies:
        copy.wait()


def per_device(nr, nz, elevation, layover, footprint_pixel, footprint_device, local_block, backscatter):
    rows, cols = elevation.shape
    tb = local_block.shape[1]
    cap = max(2, 2 * tb // (nr * nz))
    n4 = nr * cap // 2
    held = backscatter.shape[0]
    vmem = pl.BlockSpec(memory_space=pltpu.VMEM)
    hbm = pl.BlockSpec(memory_space=pltpu.HBM)
    dma = pltpu.SemaphoreType.DMA
    gamma, found, places = pl.pallas_call(
        functools.partial(exchange, nr, nz, cap),
        out_shape=(
            jax.ShapeDtypeStruct((held, PIX), F32),
            jax.ShapeDtypeStruct((tb, PIX), F32),
            jax.ShapeDtypeStruct((tb, BR * BC), jnp.int32),
        ),
        in_specs=[hbm] * 6,
        out_specs=(vmem, vmem, vmem),
        scratch_shapes=[
            pltpu.VMEM((1, tb), jnp.int32),
            pltpu.VMEM((1, tb), jnp.int32),
            pltpu.VMEM((held, PIX), F32),
            pltpu.VMEM((tb // 8, 128, BR * BC), BF16),
            pltpu.VMEM((rows + 16, cols + 256), F32),
            pltpu.VMEM((rows, cols), jnp.int32),
            pltpu.VMEM((rows, cols), jnp.int32),
            pltpu.VMEM((8, cols), F32),
            pltpu.VMEM((nz * n4, tb), BF16),
            pltpu.VMEM((nz * n4, tb), BF16),
            pltpu.VMEM((tb, nz * n4), BF16),
            pltpu.VMEM((3, 256, 3 * n4), BF16),
            pltpu.VMEM((3, 3 * 128, 128), BF16),
            pltpu.VMEM((tb, PIX), F32),
            pltpu.VMEM((2, 8, rows), F32),
            pltpu.VMEM((2, 8, rows), F32),
            pltpu.VMEM((2, nz, n4, 128), F32),
            pltpu.VMEM((2, nz, n4, 128), F32),
            pltpu.VMEM((nr, nz, 128), F32),
            pltpu.VMEM((nr, nz, 128), F32),
            pltpu.VMEM((5, nz, 128), F32),
            pltpu.VMEM((2, 2, 64, 128), F32),
            pltpu.VMEM((2, 2, 64, 128), F32),
            pltpu.VMEM((2, 64, 128), F32),
            pltpu.VMEM((2, 2, 64, 128), F32),
            pltpu.VMEM((2, nz, n4, 128), F32),
            pltpu.VMEM((2, nz, n4, 128), F32),
            pltpu.SemaphoreType.REGULAR,
            pltpu.SemaphoreType.REGULAR,
            dma((6,)),
            dma((4,)),
            dma((4,)),
            dma,
            dma,
            dma((4,)),
            dma((4,)),
            *([dma((2, 2))] * 8),
        ],
        compiler_params=pltpu.CompilerParams(
            collective_id=0, has_side_effects=True, vmem_limit_bytes=40 * 2**20
        ),
    )(
        *(
            pltpu.with_memory_space_constraint(x, pltpu.HBM)
            for x in (
                elevation, layover, footprint_pixel,
                footprint_device.reshape(1, tb), local_block, backscatter,
            )
        )
    )
    return pl.pallas_call(
        lookup,
        out_shape=(
            jax.ShapeDtypeStruct((held, PIX), F32),
            jax.ShapeDtypeStruct((rows, cols), F32),
        ),
        in_specs=[vmem, vmem, vmem],
        out_specs=(hbm, hbm),
        scratch_shapes=[pltpu.VMEM((rows, cols), F32), dma((1 + max(1, rows // 64),))],
        compiler_params=pltpu.CompilerParams(vmem_limit_bytes=8 * 2**20),
    )(found, places, gamma)


def solution(mesh):
    in_specs = (
        P("maprow", ("mapcol", "sect")),
        P("maprow", ("mapcol", "sect")),
        P("maprow", ("mapcol", "sect")),
        P(("maprow", "mapcol", "sect"), None, None),
        P(("maprow", "mapcol", "sect"), None),
        P(("maprow", "mapcol", "sect"), None),
    )
    out_specs = (P(("maprow", "mapcol", "sect"), None), P("maprow", ("mapcol", "sect")))
    return jax.shard_map(
        functools.partial(per_device, mesh.shape["maprow"], mesh.shape["mapcol"]),
        mesh=mesh,
        in_specs=in_specs,
        out_specs=out_specs,
        check_vma=False,
    )
```

```python
import functools

import jax
import jax.numpy as jnp
from jax import lax
from jax.experimental import pallas as pl
from jax.experimental.pallas import tpu as pltpu
from jax.sharding import PartitionSpec as P

BR = 16
BC = 16
PIX = 128
CELL_SPACING = 10.0
HEADING = 0.2
MESH = pl.DeviceIdType.MESH
F32 = jnp.float32
BF16 = jnp.bfloat16


def iota(shape, dim):
    return lax.broadcasted_iota(jnp.int32, shape, dim)


def iotaf(shape, dim):
    return iota(shape, dim).astype(F32)


def swap_groups(x):
    lane, row = iota((8, 128), 1), iota((8, 128), 0)
    x = pltpu.roll(x, 0, 1, stride=16, stride_axis=0)
    x = jnp.take_along_axis(x, ((lane >> 4) - row) & 7, axis=0)
    return jnp.take_along_axis(x, (lane + 16 * row) & 127, axis=1)


def split(x):
    first = x.astype(BF16)
    return jnp.concatenate([first, (x - first.astype(F32)).astype(BF16)], axis=1)


def folded(x):
    half = x.shape[1] // 2
    return x[:, :half] + x[:, half:]


def dot(a, b):
    return lax.dot_general(a, b, (((1,), (0,)), ((), ())), preferred_element_type=F32)


def dot_nt(a, b):
    return lax.dot_general(a, b, (((1,), (1,)), ((), ())), preferred_element_type=F32)


def pixel_side(pixel):
    places = [swap_groups(pixel[8 * half : 8 * half + 8]) for half in range(2)]
    lows = [
        jnp.where((p & 15)[:, None, :] == iota((8, 16, 128), 1), 1.0, 0.0).reshape(128, 128)
        for p in places
    ]
    return jnp.concatenate(places, axis=1), jnp.concatenate(lows, axis=1).astype(BF16)


def block_sums(area, places, lows):
    firsts, seconds = [], []
    for half in range(2):
        a = swap_groups(area[8 * half : 8 * half + 8])
        high = places[:, 128 * half : 128 * half + 128] >> 4
        a1 = a.astype(BF16).astype(F32)
        a2 = a - a1
        is_high = high[:, None, :] == iota((8, 8, 128), 1)
        firsts.append(jnp.where(is_high, a1[:, None, :], 0.0).reshape(64, 128))
        seconds.append(jnp.where(is_high, a2[:, None, :], 0.0).reshape(64, 128))
    left = jnp.concatenate(
        [jnp.concatenate(firsts, axis=1), jnp.concatenate(seconds, axis=1)], axis=0
    ).astype(BF16)
    out = dot_nt(left, lows)
    out = out[:64] + out[64:]
    group = iota((8, 128), 1) >> 4
    own = out[0:8]
    for b in range(1, 8):
        own = jnp.where(group == b, out[8 * b : 8 * b + 8], own)
    return swap_groups(own)


STEP = (0, 2, -2, 1, 3, -1, -3, 4)
SPANS = ((7, 8, 2), (3, 5, 1), (5, 7, -1), (0, 3, 0))
AWAY = (
    (2, 2), (1, 3), (3, 1), (2, 1), (1, 2), (3, 3), (1, 1), (2, 3),
    (3, 2), (2, 0), (0, 2), (1, 0), (3, 0), (0, 1), (0, 3), (0, 0),
)
TABLES = ((1, 4, 7), (2, 6, 7), (0, 3, 5))


def exchange(
    nr, nz, cap,
    elev, lay, pix, target_in, local_in, back_in,
    gamma, found, places,
    target, local, back, low_table, epad, layv, pixv, look, put_low, put_high, pick, oht, oh, hist,
    edge_out, edge_in, sendb, recvb, idsend, idrecv, named, partial, cin, packed, gin, backb, retb,
    plane_sem, steps_sem, in_sem, halo_send, halo_recv, id_send, id_recv, name_send, name_recv, out_send, out_recv,
    sum_send, sum_recv, gam_send, gam_recv, ret_send, ret_recv,
):
    rows, cols = elev.shape
    tb = target_in.shape[1]
    dests = nr * nz
    hc = cap // 2
    n4 = nr * hc
    tiles = cols // 128
    r, c, s = lax.axis_index("maprow"), lax.axis_index("mapcol"), lax.axis_index("sect")

    def plane(step):
        return lax.rem(c + (step + nz), nz)

    if nr == 16:
        along_x = [(r // 4 + n) % 4 * 4 for n in range(4)]
        along_y = [(r % 4 + n) % 4 for n in range(4)]
        peers = [along_x[x] + along_y[y] for x, y in AWAY]
        line_x = [along_x[n] + along_y[0] for n in (2, 1, 3)]
        line_y = [along_x[0] + along_y[n] for n in (2, 1, 3)]
    else:
        peers = [lax.rem(r + 1 + i, nr) for i in range(nr)]
        line_x, line_y = [], peers[:-1]

    west = {"mapcol": lax.rem(c + nz - 1 + s, nz), "sect": 1 - s}
    east = {"mapcol": lax.rem(c + s, nz), "sect": 1 - s}
    north, south = {"maprow": lax.rem(r + nr - 1, nr)}, {"maprow": lax.rem(r + 1, nr)}

    barrier = pltpu.get_barrier_semaphore()

    line_x = [{"maprow": i} for i in line_x]
    line_y = [{"maprow": i} for i in line_y]
    line_z = [{"mapcol": plane(step)} for step in (2, -2, 1, -1)]
    greeted = (north, south, west, east, *line_z, *line_x, *line_y)

    def greet(devices, sem):
        for device in devices:
            pl.semaphore_signal(sem, inc=1, device_id=device, device_id_type=MESH)

    greet(greeted, barrier)

    loads = [
        pltpu.make_async_copy(target_in, target, in_sem.at[0]),
        pltpu.make_async_copy(local_in, local, in_sem.at[1]),
        pltpu.make_async_copy(pix, pixv, in_sem.at[2]),
        pltpu.make_async_copy(elev, epad.at[8 : 8 + rows, 128 : 128 + cols], in_sem.at[3]),
        pltpu.make_async_copy(lay, layv, in_sem.at[4]),
        pltpu.make_async_copy(back_in, back, in_sem.at[5]),
    ]
    for load in loads:
        load.start()

    loads[0].wait()
    loads[1].wait()
    name = target[...]
    ahead = ((name & (nz - 1)) + (nz - c)) & (nz - 1)
    order = jnp.zeros((1, tb), jnp.int32)
    for p, step in enumerate(STEP):
        order = jnp.where(ahead == step % nz, p, order)
    spot = (name >> (nz.bit_length() - 1)) * nz + order
    onehot = iota((dests, tb), 0) == spot
    earlier = jnp.where(iota((tb, tb), 0) < iota((tb, tb), 1), 1.0, 0.0).astype(BF16)
    running = dot(jnp.where(onehot, 1.0, 0.0).astype(BF16), earlier)
    rank = jnp.sum(jnp.where(onehot, running, 0.0), axis=0, keepdims=True)
    slot = (spot * cap).astype(F32) + rank
    ids = jnp.where(onehot, local[...].astype(F32), 0.0).astype(BF16)
    high = rank >= float(hc)
    within = jnp.where(high, rank - float(hc), rank)
    at_lane = (r * hc).astype(F32) + within + jnp.where(high, float(n4), 0.0)
    lanes = jnp.where(iotaf((128, tb), 0) == at_lane, 1.0, 0.0).astype(BF16)
    idsend[...] = dot_nt(ids, lanes).reshape(nr, nz, 128)
    idrecv[pl.ds(r, 1)] = idsend[pl.ds(r, 1)]

    loads[3].wait()
    edge_out[0] = jnp.transpose(epad[8 : 8 + rows, 128:256])[0:8]
    edge_out[1] = jnp.transpose(epad[8 : 8 + rows, cols : 128 + cols])[120:128]

    pl.semaphore_wait(barrier, len(greeted))

    inner = slice(128, 128 + cols)
    halos = [
        (epad.at[rows + 7 : rows + 8, inner], epad.at[7:8, inner], south),
        (epad.at[8:9, inner], epad.at[rows + 8 : rows + 9, inner], north),
        (edge_out.at[0, 0:1], edge_in.at[0, 0:1], west),
        (edge_out.at[1, 7:8], edge_in.at[1, 7:8], east),
    ]
    halos = [
        pltpu.make_async_remote_copy(
            src_ref=src, dst_ref=dst, send_sem=halo_send.at[i], recv_sem=halo_recv.at[i],
            device_id=where, device_id_type=MESH,
        )
        for i, (src, dst, where) in enumerate(halos)
    ]
    for halo in halos:
        halo.start()
    greet(line_x, plane_sem)

    loads[2].wait()
    group_bands = 8 if rows % (8 * BR) == 0 else 2

    def pixels(i, carry):
        for n in range(group_bands):
            top = pl.multiple_of(i * (group_bands * BR) + n * BR, BR)
            for j in range(tiles):
                unit = i * (group_bands * tiles) + n * tiles + j
                place, low = pixel_side(pixv[pl.ds(top, BR), 128 * j : 128 * j + 128])
                places[pl.ds(pl.multiple_of(8 * unit, 8), 8), :] = place
                low_table[unit] = low
        return carry

    lax.fori_loop(0, rows // (group_bands * BR), pixels, 0)

    if line_x:
        pl.semaphore_wait(plane_sem, len(line_x))
    greet(line_z, steps_sem)

    for peer in peers[:-1]:
        pltpu.make_async_remote_copy(
            src_ref=idsend.at[peer], dst_ref=idrecv.at[r], send_sem=id_send, recv_sem=id_recv,
            device_id={"maprow": peer}, device_id_type=MESH,
        ).start()

    def to_peers(source, sink, send_sem, recv_sem, way):
        def start(span, peer):
            p0, p1, step = span
            where = plane(way * step)
            if step == 2:
                where = jnp.where((r + peer) % 2 == 0, plane(2 * way), plane(-2 * way))
            k = 0 if step == 0 else 1
            pltpu.make_async_remote_copy(
                src_ref=source(p0, p1, peer), dst_ref=sink(p0, p1, r),
                send_sem=send_sem.at[k], recv_sem=recv_sem.at[k],
                device_id={"maprow": peer, "mapcol": where}, device_id_type=MESH,
            ).start()

        for i, peer in enumerate(peers):
            for span in SPANS:
                if i < nr - 1 or span[2] != 0:
                    start(span, peer)

    def done(part, sem):
        pltpu.make_async_copy(part, part, sem).wait()

    def done_rows(buffer, sem):
        done(buffer.at[3:nz], sem.at[1])
        done(buffer.at[0:3, 0 : (nr - 1) * hc], sem.at[0])

    def of_rows(buffer):
        return lambda p0, p1, i: buffer.at[p0:p1, pl.ds(i * hc, hc)]

    i0 = iota((nz * n4, 1), 0)
    row_slot = (((i0 % n4) // hc) * (nz * cap) + (i0 // n4) * cap + i0 % hc).astype(F32)
    put_low[...] = jnp.where(row_slot == slot, 1.0, 0.0).astype(BF16)
    put_high[...] = jnp.where(row_slot + float(hc) == slot, 1.0, 0.0).astype(BF16)

    column = ((c * 2 + s) * cols + iota((1, cols), 1)).astype(F32)
    incidence = 0.52 + 0.28 * (column + 0.5) / float(cols * nz * 2)
    sine, heading = jnp.sin(incidence), jnp.full((1, cols), HEADING, F32)
    look[0:1, :] = -sine * jnp.cos(heading) / (2.0 * CELL_SPACING)
    look[1:2, :] = -sine * jnp.sin(heading) / (2.0 * CELL_SPACING)
    look[2:3, :] = jnp.cos(incidence)

    loads[4].wait()

    def unit_sums(i, j):
        lane = iota((BR, 128), 1)
        top = BR * i
        at = slice(128 * j, 128 * j + 128)
        around = epad[top : top + 32, 128 + 128 * j : 256 + 128 * j]
        before, here, after = (
            epad[top + 8 : top + 24, 128 * n : 128 * n + 128] for n in (j, j + 1, j + 2)
        )
        before = pltpu.roll(jnp.where(lane == 127, before, here), 1, 1)
        after = pltpu.roll(jnp.where(lane == 0, after, here), 127, 1)
        rise_cols = after - before
        rise_rows = around[9:25] - around[7:23]
        facing = look[2:3, at] - rise_cols * look[0:1, at] - rise_rows * look[1:2, at]
        lit = (1 - layv[top : top + BR, at]).astype(F32)
        unit = i * tiles + j
        span = slice(8 * unit, 8 * unit + 8)
        area = jnp.maximum(facing, 0.0) * lit
        hist[span, :] = block_sums(area, places[span, :], low_table[unit])

    nb = rows // BR
    inside = [(i, j) for i in range(1, nb - 1) for j in range(1, tiles - 1)]
    for i, j in inside:
        unit_sums(i, j)

    for halo in halos:
        halo.wait_recv()

    @pl.when(r == 0)
    def _():
        epad[7:8, inner] = jnp.zeros((1, cols), F32)

    @pl.when(r == nr - 1)
    def _():
        epad[rows + 8 : rows + 9, inner] = jnp.zeros((1, cols), F32)

    first, last = (c == 0) & (s == 0), (c == nz - 1) & (s == 1)
    west_edge = jnp.where(first, 0.0, edge_in[1, 7:8, :])
    east_edge = jnp.where(last, 0.0, edge_in[0, 0:1, :])
    epad[8 : 8 + rows, 0:128] = jnp.transpose(jnp.broadcast_to(west_edge, (128, rows)))
    epad[8 : 8 + rows, 128 + cols : 256 + cols] = jnp.transpose(
        jnp.broadcast_to(east_edge, (128, rows))
    )
    for i in range(nb):
        for j in range(tiles):
            if (i, j) not in inside:
                unit_sums(i, j)

    pl.semaphore_wait(steps_sem, len(line_z))

    left = iota((nz * n4, 128), 1) < 64
    sums = hist[...]
    lower = folded(dot(put_low[...], split(sums)))
    upper = folded(dot(put_high[...], split(pltpu.roll(sums, 64, 1))))
    sendb[0] = jnp.where(left, lower, upper).reshape(nz, n4, 128)
    sendb[1] = jnp.where(left, upper, lower).reshape(nz, n4, 128)
    mine = pl.ds(r * hc, hc)
    for q in range(2):
        recvb[q, 0:3, mine] = sendb[q, 0:3, mine]
        to_peers(of_rows(sendb.at[q]), of_rows(recvb.at[q]), out_send.at[q], out_recv.at[q], 1)

    done(idrecv.at[0 : nr - 1], id_recv)
    names = idrecv[0]
    for i in range(1, nr):
        names = names + idrecv[i]
    named[0] = names
    tells = [
        pltpu.make_async_remote_copy(
            src_ref=named.at[0], dst_ref=named.at[n + 1],
            send_sem=name_send.at[n], recv_sem=name_recv.at[n],
            device_id={"mapcol": plane(step)}, device_id_type=MESH,
        )
        for n, step in enumerate((1, -1, 2, -2))
    ]
    for tell in tells:
        tell.start()

    row_of = (
        within
        + (((spot & (nz - 1)) * nr + (spot >> (nz.bit_length() - 1))) * hc).astype(F32)
        + jnp.where(high, float(nz * n4), 0.0)
    )
    row_down = jnp.transpose(jnp.broadcast_to(row_of, (128, tb)))
    high_down = row_down >= float(nz * n4)
    row_down = jnp.where(high_down, row_down - float(nz * n4), row_down)
    for n in range(0, nz * n4, 128):
        width = min(128, nz * n4 - n)
        pick[:, n : n + width] = jnp.where(
            row_down[:, :width] == iotaf((1, width), 1) + float(n), 1.0, 0.0
        ).astype(BF16)

    loads[5].wait()
    for tell in tells:
        tell.wait_recv()
    from_step = (0, 0, 0, 1, 1, 2, 2)
    lane = iota((1, 128), 1)
    even = ((lane % n4) // hc + r) % 2 == 0
    for t, table in enumerate(TABLES):
        asked = []
        for m, p in enumerate(table):
            name = named[from_step[p] if p < 7 else 3 + t, p : p + 1, :]
            if p == 7:
                name = jnp.where(even == (t == 0), name, -1.0)
            asked.append(name)
            if 2 * n4 < 128:
                name = jnp.where(lane < 2 * n4, name, -1.0)
            wide = jnp.broadcast_to(name, (128, 128))
            at = slice(128 * m, 128 * m + 128)
            oh[t, at, :] = jnp.where(
                jnp.transpose(wide) == iotaf((128, 128), 1), 1.0, 0.0
            ).astype(BF16)
        for half_at in range(2):
            name = jnp.concatenate([x[:, n4 * half_at : n4 * half_at + n4] for x in asked], axis=1)
            oht[t, 128 * half_at : 128 * half_at + 128, :] = jnp.where(
                iotaf((128, 3 * n4), 0) == name, 1.0, 0.0
            ).astype(BF16)
    half = iota((64, 128), 1) < 64
    backs = [back[0:64, :], back[64:128, :]]
    backs = [
        jnp.where(half, backs[0], pltpu.roll(backs[1], 64, 1)),
        jnp.where(half, pltpu.roll(backs[0], 64, 1), backs[1]),
    ]

    whole_half = iota((128, 128), 1) < 64

    def table_of(q, t):
        given = jnp.concatenate([split(recvb[q, p]) for p in TABLES[t]], axis=0)
        both = folded(dot(oht[t], given))
        low, high = both[0:128], both[128:256]
        total = jnp.where(whole_half, low, high) if q == 0 else jnp.where(whole_half, high, low)
        total = total + pltpu.roll(total, 64, 1)
        return jnp.where(half, total[0:64], total[64:128])

    def two_steps(source, sink, send_sem, recv_sem, way):
        return pltpu.make_async_remote_copy(
            src_ref=source, dst_ref=sink.at[way],
            send_sem=send_sem.at[way], recv_sem=recv_sem.at[way],
            device_id={"mapcol": plane((2, -2)[way])}, device_id_type=MESH,
        )

    hops = []
    own = []
    for q in range(2):
        done_rows(recvb.at[q], out_recv.at[q])
        for way in range(2):
            partial[q, way] = table_of(q, way)
            hops.append(
                two_steps(partial.at[q, way], cin.at[q], sum_send.at[q], sum_recv.at[q], way)
            )
            hops[-1].start()
        own.append(table_of(q, 2))
    gammas = []
    for q in range(2):
        hops[2 * q].wait_recv()
        hops[2 * q + 1].wait_recv()
        total = own[q] + cin[q, 0] + cin[q, 1]
        packed[q] = backs[q] / jnp.maximum(total, 1.0)
        for way in range(2):
            gammas.append(
                two_steps(packed.at[q], gin.at[q], gam_send.at[q], gam_recv.at[q], way)
            )
            gammas[-1].start()
    halves = [(packed[q], pltpu.roll(packed[q], 64, 1)) for q in range(2)]
    gamma[0:64] = jnp.where(half, halves[0][0], halves[1][1])
    gamma[64:128] = jnp.where(half, halves[0][1], halves[1][0])

    def served(q, t):
        x = packed[q] if t == 2 else gin[q, 1 - t]
        y = pltpu.roll(x, 64, 1)
        whole = jnp.concatenate([jnp.where(half, x, y), jnp.where(half, y, x)], axis=0)
        asked = folded(dot(oh[t], split(whole)))
        slots = iota((n4, 128), 1) < 64
        return [
            jnp.where(
                slots, asked[128 * m : 128 * m + n4], asked[128 * m + n4 : 128 * m + 2 * n4]
            )
            for m in range(3)
        ]

    for q in range(2):
        for p, x in zip(TABLES[2], served(q, 2)):
            backb[q, p] = x
    for q in range(2):
        gammas[2 * q].wait_recv()
        gammas[2 * q + 1].wait_recv()
        ahead_rows, behind_rows = served(q, 0), served(q, 1)
        backb[q, 1], backb[q, 4] = ahead_rows[0], ahead_rows[1]
        backb[q, 2], backb[q, 6] = behind_rows[0], behind_rows[1]
        backb[q, 7] = ahead_rows[2] + behind_rows[2]
        retb[q, 0:3, mine] = backb[q, 0:3, mine]
        to_peers(of_rows(backb.at[q]), of_rows(retb.at[q]), ret_send.at[q], ret_recv.at[q], -1)

    left = iota((tb, 128), 1) < 64
    for q in range(2):
        done_rows(retb.at[q], ret_recv.at[q])
        x = folded(dot(pick[...], split(retb[q].reshape(nz * n4, 128))))
        y = pltpu.roll(x, 64, 1)
        if q == 0:
            found[...] = jnp.where(high_down, y, x)
        else:
            found[...] = jnp.where(left, found[...], jnp.where(high_down, x, y))

    for halo in halos:
        halo.wait_send()
    done(idsend.at[0 : nr - 1], id_send)
    for tell in tells:
        tell.wait_send()
    for q in range(2):
        done_rows(sendb.at[q], out_send.at[q])
        done_rows(backb.at[q], ret_send.at[q])
    for one in (*hops, *gammas):
        one.wait_send()


def lookup(found, places, gamma, gamma_out, out, cells, sems):
    rows, cols = out.shape
    tiles = cols // 128
    chunk = 64 if rows % 64 == 0 else rows
    copies = [pltpu.make_async_copy(gamma, gamma_out, sems.at[0])]
    copies[0].start()
    for k in range(rows // chunk):
        for unit in range(k * (chunk // BR) * tiles, (k + 1) * (chunk // BR) * tiles):
            span = slice(8 * unit, 8 * unit + 8)
            for half in range(2):
                place = places[span, 128 * half : 128 * half + 128]
                top, at = BR * (unit // tiles) + 8 * half, 128 * (unit % tiles)
                cells[top : top + 8, at : at + 128] = jnp.take_along_axis(
                    found[span, :], place, axis=1
                )
        for top in range(k * chunk, (k + 1) * chunk, 8):
            for at in range(0, cols, 128):
                piece = (slice(top, top + 8), slice(at, at + 128))
                cells[piece] = swap_groups(cells[piece])
        part = slice(k * chunk, (k + 1) * chunk)
        copies.append(pltpu.make_async_copy(cells.at[part], out.at[part], sems.at[k + 1]))
        copies[-1].start()
    for copy in copies:
        copy.wait()


def per_device(nr, nz, elevation, layover, footprint_pixel, footprint_device, local_block, backscatter):
    rows, cols = elevation.shape
    tb = local_block.shape[1]
    cap = max(2, 2 * tb // (nr * nz))
    n4 = nr * cap // 2
    held = backscatter.shape[0]
    vmem = pl.BlockSpec(memory_space=pltpu.VMEM)
    hbm = pl.BlockSpec(memory_space=pltpu.HBM)
    dma = pltpu.SemaphoreType.DMA
    gamma, found, places = pl.pallas_call(
        functools.partial(exchange, nr, nz, cap),
        out_shape=(
            jax.ShapeDtypeStruct((held, PIX), F32),
            jax.ShapeDtypeStruct((tb, PIX), F32),
            jax.ShapeDtypeStruct((tb, BR * BC), jnp.int32),
        ),
        in_specs=[hbm] * 6,
        out_specs=(vmem, vmem, vmem),
        scratch_shapes=[
            pltpu.VMEM((1, tb), jnp.int32),
            pltpu.VMEM((1, tb), jnp.int32),
            pltpu.VMEM((held, PIX), F32),
            pltpu.VMEM((tb // 8, 128, BR * BC), BF16),
            pltpu.VMEM((rows + 16, cols + 256), F32),
            pltpu.VMEM((rows, cols), jnp.int32),
            pltpu.VMEM((rows, cols), jnp.int32),
            pltpu.VMEM((8, cols), F32),
            pltpu.VMEM((nz * n4, tb), BF16),
            pltpu.VMEM((nz * n4, tb), BF16),
            pltpu.VMEM((tb, nz * n4), BF16),
            pltpu.VMEM((3, 256, 3 * n4), BF16),
            pltpu.VMEM((3, 3 * 128, 128), BF16),
            pltpu.VMEM((tb, PIX), F32),
            pltpu.VMEM((2, 8, rows), F32),
            pltpu.VMEM((2, 8, rows), F32),
            pltpu.VMEM((2, nz, n4, 128), F32),
            pltpu.VMEM((2, nz, n4, 128), F32),
            pltpu.VMEM((nr, nz, 128), F32),
            pltpu.VMEM((nr, nz, 128), F32),
            pltpu.VMEM((5, nz, 128), F32),
            pltpu.VMEM((2, 2, 64, 128), F32),
            pltpu.VMEM((2, 2, 64, 128), F32),
            pltpu.VMEM((2, 64, 128), F32),
            pltpu.VMEM((2, 2, 64, 128), F32),
            pltpu.VMEM((2, nz, n4, 128), F32),
            pltpu.VMEM((2, nz, n4, 128), F32),
            pltpu.SemaphoreType.REGULAR,
            pltpu.SemaphoreType.REGULAR,
            dma((6,)),
            dma((4,)),
            dma((4,)),
            dma,
            dma,
            dma((4,)),
            dma((4,)),
            *([dma((2, 2))] * 8),
        ],
        compiler_params=pltpu.CompilerParams(
            collective_id=0, has_side_effects=True, vmem_limit_bytes=40 * 2**20
        ),
    )(
        *(
            pltpu.with_memory_space_constraint(x, pltpu.HBM)
            for x in (
                elevation, layover, footprint_pixel,
                footprint_device.reshape(1, tb), local_block, backscatter,
            )
        )
    )
    return pl.pallas_call(
        lookup,
        out_shape=(
            jax.ShapeDtypeStruct((held, PIX), F32),
            jax.ShapeDtypeStruct((rows, cols), F32),
        ),
        in_specs=[vmem, vmem, vmem],
        out_specs=(hbm, hbm),
        scratch_shapes=[pltpu.VMEM((rows, cols), F32), dma((1 + max(1, rows // 64),))],
        compiler_params=pltpu.CompilerParams(vmem_limit_bytes=8 * 2**20),
    )(found, places, gamma)


def solution(mesh):
    in_specs = (
        P("maprow", ("mapcol", "sect")),
        P("maprow", ("mapcol", "sect")),
        P("maprow", ("mapcol", "sect")),
        P(("maprow", "mapcol", "sect"), None, None),
        P(("maprow", "mapcol", "sect"), None),
        P(("maprow", "mapcol", "sect"), None),
    )
    out_specs = (P(("maprow", "mapcol", "sect"), None), P("maprow", ("mapcol", "sect")))
    return jax.shard_map(
        functools.partial(per_device, mesh.shape["maprow"], mesh.shape["mapcol"]),
        mesh=mesh,
        in_specs=in_specs,
        out_specs=out_specs,
        check_vma=False,
    )
```

```python
import functools

import jax
import jax.numpy as jnp
from jax import lax
from jax.experimental import pallas as pl
from jax.experimental.pallas import tpu as pltpu
from jax.sharding import PartitionSpec as P

BR = 16
BC = 16
PIX = 128
CELL_SPACING = 10.0
HEADING = 0.2
MESH = pl.DeviceIdType.MESH
F32 = jnp.float32
BF16 = jnp.bfloat16


def iota(shape, dim):
    return lax.broadcasted_iota(jnp.int32, shape, dim)


def iotaf(shape, dim):
    return iota(shape, dim).astype(F32)


def swap_groups(x):
    lane, row = iota((8, 128), 1), iota((8, 128), 0)
    x = pltpu.roll(x, 0, 1, stride=16, stride_axis=0)
    x = jnp.take_along_axis(x, ((lane >> 4) - row) & 7, axis=0)
    return jnp.take_along_axis(x, (lane + 16 * row) & 127, axis=1)


def split(x):
    first = x.astype(BF16)
    return jnp.concatenate([first, (x - first.astype(F32)).astype(BF16)], axis=1)


def folded(x):
    half = x.shape[1] // 2
    return x[:, :half] + x[:, half:]


def dot(a, b):
    return lax.dot_general(a, b, (((1,), (0,)), ((), ())), preferred_element_type=F32)


def dot_nt(a, b):
    return lax.dot_general(a, b, (((1,), (1,)), ((), ())), preferred_element_type=F32)


def pixel_side(pixel):
    places = [swap_groups(pixel[8 * half : 8 * half + 8]) for half in range(2)]
    lows = [
        jnp.where((p & 15)[:, None, :] == iota((8, 16, 128), 1), 1.0, 0.0).reshape(128, 128)
        for p in places
    ]
    return jnp.concatenate(places, axis=1), jnp.concatenate(lows, axis=1).astype(BF16)


def block_sums(area, places, lows):
    firsts, seconds = [], []
    for half in range(2):
        a = swap_groups(area[8 * half : 8 * half + 8])
        high = places[:, 128 * half : 128 * half + 128] >> 4
        a1 = a.astype(BF16).astype(F32)
        a2 = a - a1
        is_high = high[:, None, :] == iota((8, 8, 128), 1)
        firsts.append(jnp.where(is_high, a1[:, None, :], 0.0).reshape(64, 128))
        seconds.append(jnp.where(is_high, a2[:, None, :], 0.0).reshape(64, 128))
    left = jnp.concatenate(
        [jnp.concatenate(firsts, axis=1), jnp.concatenate(seconds, axis=1)], axis=0
    ).astype(BF16)
    out = dot_nt(left, lows)
    out = out[:64] + out[64:]
    group = iota((8, 128), 1) >> 4
    own = out[0:8]
    for b in range(1, 8):
        own = jnp.where(group == b, out[8 * b : 8 * b + 8], own)
    return swap_groups(own)


STEP = (0, 2, -2, 1, 3, -1, -3, 4)
SPANS = ((7, 8, 2), (3, 5, 1), (5, 7, -1), (0, 3, 0))
AWAY = (
    (2, 2), (1, 3), (3, 1), (2, 1), (1, 2), (3, 3), (1, 1), (2, 3),
    (3, 2), (2, 0), (0, 2), (1, 0), (3, 0), (0, 1), (0, 3), (0, 0),
)
TABLES = ((1, 4, 7), (2, 6, 7), (0, 3, 5))


def exchange(
    nr, nz, cap,
    elev, lay, pix, target_in, local_in, back_in,
    gamma, found, places,
    target, local, back, low_table, epad, layv, pixv, look, put_low, put_high, pick, oht, oh, hist,
    edge_out, edge_in, sendb, recvb, idsend, idrecv, named, partial, cin, packed, gin, backb, retb,
    plane_sem, steps_sem, in_sem, halo_send, halo_recv, id_send, id_recv, name_send, name_recv, out_send, out_recv,
    sum_send, sum_recv, gam_send, gam_recv, ret_send, ret_recv,
):
    rows, cols = elev.shape
    tb = target_in.shape[1]
    dests = nr * nz
    hc = cap // 2
    n4 = nr * hc
    tiles = cols // 128
    r, c, s = lax.axis_index("maprow"), lax.axis_index("mapcol"), lax.axis_index("sect")

    def plane(step):
        return lax.rem(c + (step + nz), nz)

    if nr == 16:
        along_x = [(r // 4 + n) % 4 * 4 for n in range(4)]
        along_y = [(r % 4 + n) % 4 for n in range(4)]
        peers = [along_x[x] + along_y[y] for x, y in AWAY]
        line_x = [along_x[n] + along_y[0] for n in (2, 1, 3)]
        line_y = [along_x[0] + along_y[n] for n in (2, 1, 3)]
    else:
        peers = [lax.rem(r + 1 + i, nr) for i in range(nr)]
        line_x, line_y = [], peers[:-1]

    west = {"mapcol": lax.rem(c + nz - 1 + s, nz), "sect": 1 - s}
    east = {"mapcol": lax.rem(c + s, nz), "sect": 1 - s}
    north, south = {"maprow": lax.rem(r + nr - 1, nr)}, {"maprow": lax.rem(r + 1, nr)}

    barrier = pltpu.get_barrier_semaphore()

    line_x = [{"maprow": i} for i in line_x]
    line_y = [{"maprow": i} for i in line_y]
    line_z = [{"mapcol": plane(step)} for step in (2, -2, 1, -1)]
    greeted = (north, south, west, east, *line_z, *line_x, *line_y)

    def greet(devices, sem):
        for device in devices:
            pl.semaphore_signal(sem, inc=1, device_id=device, device_id_type=MESH)

    greet(greeted, barrier)

    loads = [
        pltpu.make_async_copy(target_in, target, in_sem.at[0]),
        pltpu.make_async_copy(local_in, local, in_sem.at[1]),
        pltpu.make_async_copy(pix, pixv, in_sem.at[2]),
        pltpu.make_async_copy(elev, epad.at[8 : 8 + rows, 128 : 128 + cols], in_sem.at[3]),
        pltpu.make_async_copy(lay, layv, in_sem.at[4]),
        pltpu.make_async_copy(back_in, back, in_sem.at[5]),
    ]
    for i in (0, 1, 3, 2, 4, 5):
        loads[i].start()

    loads[0].wait()
    loads[1].wait()
    name = target[...]
    ahead = ((name & (nz - 1)) + (nz - c)) & (nz - 1)
    order = jnp.zeros((1, tb), jnp.int32)
    for p, step in enumerate(STEP):
        order = jnp.where(ahead == step % nz, p, order)
    spot = (name >> (nz.bit_length() - 1)) * nz + order
    onehot = iota((dests, tb), 0) == spot
    earlier = jnp.where(iota((tb, tb), 0) < iota((tb, tb), 1), 1.0, 0.0).astype(BF16)
    running = dot(jnp.where(onehot, 1.0, 0.0).astype(BF16), earlier)
    rank = jnp.sum(jnp.where(onehot, running, 0.0), axis=0, keepdims=True)
    slot = (spot * cap).astype(F32) + rank
    ids = jnp.where(onehot, local[...].astype(F32), 0.0).astype(BF16)
    high = rank >= float(hc)
    within = jnp.where(high, rank - float(hc), rank)
    at_lane = (r * hc).astype(F32) + within + jnp.where(high, float(n4), 0.0)
    lanes = jnp.where(iotaf((128, tb), 0) == at_lane, 1.0, 0.0).astype(BF16)
    idsend[...] = dot_nt(ids, lanes).reshape(nr, nz, 128)
    idrecv[pl.ds(r, 1)] = idsend[pl.ds(r, 1)]

    loads[3].wait()
    edge_out[0] = jnp.transpose(epad[8 : 8 + rows, 128:256])[0:8]
    edge_out[1] = jnp.transpose(epad[8 : 8 + rows, cols : 128 + cols])[120:128]

    pl.semaphore_wait(barrier, len(greeted))

    inner = slice(128, 128 + cols)
    halos = [
        (epad.at[rows + 7 : rows + 8, inner], epad.at[7:8, inner], south),
        (epad.at[8:9, inner], epad.at[rows + 8 : rows + 9, inner], north),
        (edge_out.at[0, 0:1], edge_in.at[0, 0:1], west),
        (edge_out.at[1, 7:8], edge_in.at[1, 7:8], east),
    ]
    halos = [
        pltpu.make_async_remote_copy(
            src_ref=src, dst_ref=dst, send_sem=halo_send.at[i], recv_sem=halo_recv.at[i],
            device_id=where, device_id_type=MESH,
        )
        for i, (src, dst, where) in enumerate(halos)
    ]
    for halo in halos:
        halo.start()
    greet(line_x, plane_sem)

    loads[2].wait()
    group_bands = 8 if rows % (8 * BR) == 0 else 2

    def pixels(i, carry):
        for n in range(group_bands):
            top = pl.multiple_of(i * (group_bands * BR) + n * BR, BR)
            for j in range(tiles):
                unit = i * (group_bands * tiles) + n * tiles + j
                place, low = pixel_side(pixv[pl.ds(top, BR), 128 * j : 128 * j + 128])
                places[pl.ds(pl.multiple_of(8 * unit, 8), 8), :] = place
                low_table[unit] = low
        return carry

    lax.fori_loop(0, rows // (group_bands * BR), pixels, 0)

    if line_x:
        pl.semaphore_wait(plane_sem, len(line_x))
    greet(line_z, steps_sem)

    for peer in peers[:-1]:
        pltpu.make_async_remote_copy(
            src_ref=idsend.at[peer], dst_ref=idrecv.at[r], send_sem=id_send, recv_sem=id_recv,
            device_id={"maprow": peer}, device_id_type=MESH,
        ).start()

    def to_peers(source, sink, send_sem, recv_sem, way):
        def start(span, peer):
            p0, p1, step = span
            where = plane(way * step)
            if step == 2:
                where = jnp.where((r + peer) % 2 == 0, plane(2 * way), plane(-2 * way))
            k = 0 if step == 0 else 1
            pltpu.make_async_remote_copy(
                src_ref=source(p0, p1, peer), dst_ref=sink(p0, p1, r),
                send_sem=send_sem.at[k], recv_sem=recv_sem.at[k],
                device_id={"maprow": peer, "mapcol": where}, device_id_type=MESH,
            ).start()

        for i, peer in enumerate(peers):
            for span in SPANS:
                if i < nr - 1 or span[2] != 0:
                    start(span, peer)

    def done(part, sem):
        pltpu.make_async_copy(part, part, sem).wait()

    def done_rows(buffer, sem):
        done(buffer.at[3:nz], sem.at[1])
        done(buffer.at[0:3, 0 : (nr - 1) * hc], sem.at[0])

    def of_rows(buffer):
        return lambda p0, p1, i: buffer.at[p0:p1, pl.ds(i * hc, hc)]

    i0 = iota((nz * n4, 1), 0)
    row_slot = (((i0 % n4) // hc) * (nz * cap) + (i0 // n4) * cap + i0 % hc).astype(F32)
    put_low[...] = jnp.where(row_slot == slot, 1.0, 0.0).astype(BF16)
    put_high[...] = jnp.where(row_slot + float(hc) == slot, 1.0, 0.0).astype(BF16)

    column = ((c * 2 + s) * cols + iota((1, cols), 1)).astype(F32)
    incidence = 0.52 + 0.28 * (column + 0.5) / float(cols * nz * 2)
    sine, heading = jnp.sin(incidence), jnp.full((1, cols), HEADING, F32)
    look[0:1, :] = -sine * jnp.cos(heading) / (2.0 * CELL_SPACING)
    look[1:2, :] = -sine * jnp.sin(heading) / (2.0 * CELL_SPACING)
    look[2:3, :] = jnp.cos(incidence)

    loads[4].wait()

    def unit_sums(i, j):
        lane = iota((BR, 128), 1)
        top = BR * i
        at = slice(128 * j, 128 * j + 128)
        around = epad[top : top + 32, 128 + 128 * j : 256 + 128 * j]
        before, here, after = (
            epad[top + 8 : top + 24, 128 * n : 128 * n + 128] for n in (j, j + 1, j + 2)
        )
        before = pltpu.roll(jnp.where(lane == 127, before, here), 1, 1)
        after = pltpu.roll(jnp.where(lane == 0, after, here), 127, 1)
        rise_cols = after - before
        rise_rows = around[9:25] - around[7:23]
        facing = look[2:3, at] - rise_cols * look[0:1, at] - rise_rows * look[1:2, at]
        lit = (1 - layv[top : top + BR, at]).astype(F32)
        unit = i * tiles + j
        span = slice(8 * unit, 8 * unit + 8)
        area = jnp.maximum(facing, 0.0) * lit
        hist[span, :] = block_sums(area, places[span, :], low_table[unit])

    nb = rows // BR
    inside = [(i, j) for i in range(1, nb - 1) for j in range(1, tiles - 1)]
    for i, j in inside:
        unit_sums(i, j)

    for halo in halos:
        halo.wait_recv()

    @pl.when(r == 0)
    def _():
        epad[7:8, inner] = jnp.zeros((1, cols), F32)

    @pl.when(r == nr - 1)
    def _():
        epad[rows + 8 : rows + 9, inner] = jnp.zeros((1, cols), F32)

    first, last = (c == 0) & (s == 0), (c == nz - 1) & (s == 1)
    west_edge = jnp.where(first, 0.0, edge_in[1, 7:8, :])
    east_edge = jnp.where(last, 0.0, edge_in[0, 0:1, :])
    epad[8 : 8 + rows, 0:128] = jnp.transpose(jnp.broadcast_to(west_edge, (128, rows)))
    epad[8 : 8 + rows, 128 + cols : 256 + cols] = jnp.transpose(
        jnp.broadcast_to(east_edge, (128, rows))
    )
    for i in range(nb):
        for j in range(tiles):
            if (i, j) not in inside:
                unit_sums(i, j)

    pl.semaphore_wait(steps_sem, len(line_z))

    left = iota((nz * n4, 128), 1) < 64
    sums = hist[...]
    lower = folded(dot(put_low[...], split(sums)))
    upper = folded(dot(put_high[...], split(pltpu.roll(sums, 64, 1))))
    sendb[0] = jnp.where(left, lower, upper).reshape(nz, n4, 128)
    sendb[1] = jnp.where(left, upper, lower).reshape(nz, n4, 128)
    mine = pl.ds(r * hc, hc)
    for q in range(2):
        recvb[q, 0:3, mine] = sendb[q, 0:3, mine]
        to_peers(of_rows(sendb.at[q]), of_rows(recvb.at[q]), out_send.at[q], out_recv.at[q], 1)

    done(idrecv.at[0 : nr - 1], id_recv)
    names = idrecv[0]
    for i in range(1, nr):
        names = names + idrecv[i]
    named[0] = names
    tells = [
        pltpu.make_async_remote_copy(
            src_ref=named.at[0], dst_ref=named.at[n + 1],
            send_sem=name_send.at[n], recv_sem=name_recv.at[n],
            device_id={"mapcol": plane(step)}, device_id_type=MESH,
        )
        for n, step in enumerate((1, -1, 2, -2))
    ]
    for tell in tells:
        tell.start()

    row_of = (
        within
        + (((spot & (nz - 1)) * nr + (spot >> (nz.bit_length() - 1))) * hc).astype(F32)
        + jnp.where(high, float(nz * n4), 0.0)
    )
    row_down = jnp.transpose(jnp.broadcast_to(row_of, (128, tb)))
    high_down = row_down >= float(nz * n4)
    row_down = jnp.where(high_down, row_down - float(nz * n4), row_down)
    for n in range(0, nz * n4, 128):
        width = min(128, nz * n4 - n)
        pick[:, n : n + width] = jnp.where(
            row_down[:, :width] == iotaf((1, width), 1) + float(n), 1.0, 0.0
        ).astype(BF16)

    loads[5].wait()
    for tell in tells:
        tell.wait_recv()
    from_step = (0, 0, 0, 1, 1, 2, 2)
    lane = iota((1, 128), 1)
    even = ((lane % n4) // hc + r) % 2 == 0
    for t, table in enumerate(TABLES):
        asked = []
        for m, p in enumerate(table):
            name = named[from_step[p] if p < 7 else 3 + t, p : p + 1, :]
            if p == 7:
                name = jnp.where(even == (t == 0), name, -1.0)
            asked.append(name)
            if 2 * n4 < 128:
                name = jnp.where(lane < 2 * n4, name, -1.0)
            wide = jnp.broadcast_to(name, (128, 128))
            at = slice(128 * m, 128 * m + 128)
            oh[t, at, :] = jnp.where(
                jnp.transpose(wide) == iotaf((128, 128), 1), 1.0, 0.0
            ).astype(BF16)
        for half_at in range(2):
            name = jnp.concatenate([x[:, n4 * half_at : n4 * half_at + n4] for x in asked], axis=1)
            oht[t, 128 * half_at : 128 * half_at + 128, :] = jnp.where(
                iotaf((128, 3 * n4), 0) == name, 1.0, 0.0
            ).astype(BF16)
    half = iota((64, 128), 1) < 64
    backs = [back[0:64, :], back[64:128, :]]
    backs = [
        jnp.where(half, backs[0], pltpu.roll(backs[1], 64, 1)),
        jnp.where(half, pltpu.roll(backs[0], 64, 1), backs[1]),
    ]

    whole_half = iota((128, 128), 1) < 64

    def table_of(q, t):
        given = jnp.concatenate([split(recvb[q, p]) for p in TABLES[t]], axis=0)
        both = folded(dot(oht[t], given))
        low, high = both[0:128], both[128:256]
        total = jnp.where(whole_half, low, high) if q == 0 else jnp.where(whole_half, high, low)
        total = total + pltpu.roll(total, 64, 1)
        return jnp.where(half, total[0:64], total[64:128])

    def two_steps(source, sink, send_sem, recv_sem, way):
        return pltpu.make_async_remote_copy(
            src_ref=source, dst_ref=sink.at[way],
            send_sem=send_sem.at[way], recv_sem=recv_sem.at[way],
            device_id={"mapcol": plane((2, -2)[way])}, device_id_type=MESH,
        )

    hops = []
    own = []
    for q in range(2):
        done_rows(recvb.at[q], out_recv.at[q])
        for way in range(2):
            partial[q, way] = table_of(q, way)
            hops.append(
                two_steps(partial.at[q, way], cin.at[q], sum_send.at[q], sum_recv.at[q], way)
            )
            hops[-1].start()
        own.append(table_of(q, 2))
    gammas = []
    for q in range(2):
        hops[2 * q].wait_recv()
        hops[2 * q + 1].wait_recv()
        total = own[q] + cin[q, 0] + cin[q, 1]
        packed[q] = backs[q] / jnp.maximum(total, 1.0)
        for way in range(2):
            gammas.append(
                two_steps(packed.at[q], gin.at[q], gam_send.at[q], gam_recv.at[q], way)
            )
            gammas[-1].start()
    halves = [(packed[q], pltpu.roll(packed[q], 64, 1)) for q in range(2)]
    gamma[0:64] = jnp.where(half, halves[0][0], halves[1][1])
    gamma[64:128] = jnp.where(half, halves[0][1], halves[1][0])

    def served(q, t):
        x = packed[q] if t == 2 else gin[q, 1 - t]
        y = pltpu.roll(x, 64, 1)
        whole = jnp.concatenate([jnp.where(half, x, y), jnp.where(half, y, x)], axis=0)
        asked = folded(dot(oh[t], split(whole)))
        slots = iota((n4, 128), 1) < 64
        return [
            jnp.where(
                slots, asked[128 * m : 128 * m + n4], asked[128 * m + n4 : 128 * m + 2 * n4]
            )
            for m in range(3)
        ]

    for q in range(2):
        for p, x in zip(TABLES[2], served(q, 2)):
            backb[q, p] = x
    for q in range(2):
        gammas[2 * q].wait_recv()
        gammas[2 * q + 1].wait_recv()
        ahead_rows, behind_rows = served(q, 0), served(q, 1)
        backb[q, 1], backb[q, 4] = ahead_rows[0], ahead_rows[1]
        backb[q, 2], backb[q, 6] = behind_rows[0], behind_rows[1]
        backb[q, 7] = ahead_rows[2] + behind_rows[2]
        retb[q, 0:3, mine] = backb[q, 0:3, mine]
        to_peers(of_rows(backb.at[q]), of_rows(retb.at[q]), ret_send.at[q], ret_recv.at[q], -1)

    left = iota((tb, 128), 1) < 64
    for q in range(2):
        done_rows(retb.at[q], ret_recv.at[q])
        x = folded(dot(pick[...], split(retb[q].reshape(nz * n4, 128))))
        y = pltpu.roll(x, 64, 1)
        if q == 0:
            found[...] = jnp.where(high_down, y, x)
        else:
            found[...] = jnp.where(left, found[...], jnp.where(high_down, x, y))

    for halo in halos:
        halo.wait_send()
    done(idsend.at[0 : nr - 1], id_send)
    for tell in tells:
        tell.wait_send()
    for q in range(2):
        done_rows(sendb.at[q], out_send.at[q])
        done_rows(backb.at[q], ret_send.at[q])
    for one in (*hops, *gammas):
        one.wait_send()


def lookup(found, places, gamma, gamma_out, out, cells, sems):
    rows, cols = out.shape
    tiles = cols // 128
    chunk = 64 if rows % 64 == 0 else rows
    copies = [pltpu.make_async_copy(gamma, gamma_out, sems.at[0])]
    copies[0].start()
    for k in range(rows // chunk):
        for unit in range(k * (chunk // BR) * tiles, (k + 1) * (chunk // BR) * tiles):
            span = slice(8 * unit, 8 * unit + 8)
            for half in range(2):
                place = places[span, 128 * half : 128 * half + 128]
                top, at = BR * (unit // tiles) + 8 * half, 128 * (unit % tiles)
                cells[top : top + 8, at : at + 128] = jnp.take_along_axis(
                    found[span, :], place, axis=1
                )
        for top in range(k * chunk, (k + 1) * chunk, 8):
            for at in range(0, cols, 128):
                piece = (slice(top, top + 8), slice(at, at + 128))
                cells[piece] = swap_groups(cells[piece])
        part = slice(k * chunk, (k + 1) * chunk)
        copies.append(pltpu.make_async_copy(cells.at[part], out.at[part], sems.at[k + 1]))
        copies[-1].start()
    for copy in copies:
        copy.wait()


def per_device(nr, nz, elevation, layover, footprint_pixel, footprint_device, local_block, backscatter):
    rows, cols = elevation.shape
    tb = local_block.shape[1]
    cap = max(2, 2 * tb // (nr * nz))
    n4 = nr * cap // 2
    held = backscatter.shape[0]
    vmem = pl.BlockSpec(memory_space=pltpu.VMEM)
    hbm = pl.BlockSpec(memory_space=pltpu.HBM)
    dma = pltpu.SemaphoreType.DMA
    gamma, found, places = pl.pallas_call(
        functools.partial(exchange, nr, nz, cap),
        out_shape=(
            jax.ShapeDtypeStruct((held, PIX), F32),
            jax.ShapeDtypeStruct((tb, PIX), F32),
            jax.ShapeDtypeStruct((tb, BR * BC), jnp.int32),
        ),
        in_specs=[hbm] * 6,
        out_specs=(vmem, vmem, vmem),
        scratch_shapes=[
            pltpu.VMEM((1, tb), jnp.int32),
            pltpu.VMEM((1, tb), jnp.int32),
            pltpu.VMEM((held, PIX), F32),
            pltpu.VMEM((tb // 8, 128, BR * BC), BF16),
            pltpu.VMEM((rows + 16, cols + 256), F32),
            pltpu.VMEM((rows, cols), jnp.int32),
            pltpu.VMEM((rows, cols), jnp.int32),
            pltpu.VMEM((8, cols), F32),
            pltpu.VMEM((nz * n4, tb), BF16),
            pltpu.VMEM((nz * n4, tb), BF16),
            pltpu.VMEM((tb, nz * n4), BF16),
            pltpu.VMEM((3, 256, 3 * n4), BF16),
            pltpu.VMEM((3, 3 * 128, 128), BF16),
            pltpu.VMEM((tb, PIX), F32),
            pltpu.VMEM((2, 8, rows), F32),
            pltpu.VMEM((2, 8, rows), F32),
            pltpu.VMEM((2, nz, n4, 128), F32),
            pltpu.VMEM((2, nz, n4, 128), F32),
            pltpu.VMEM((nr, nz, 128), F32),
            pltpu.VMEM((nr, nz, 128), F32),
            pltpu.VMEM((5, nz, 128), F32),
            pltpu.VMEM((2, 2, 64, 128), F32),
            pltpu.VMEM((2, 2, 64, 128), F32),
            pltpu.VMEM((2, 64, 128), F32),
            pltpu.VMEM((2, 2, 64, 128), F32),
            pltpu.VMEM((2, nz, n4, 128), F32),
            pltpu.VMEM((2, nz, n4, 128), F32),
            pltpu.SemaphoreType.REGULAR,
            pltpu.SemaphoreType.REGULAR,
            dma((6,)),
            dma((4,)),
            dma((4,)),
            dma,
            dma,
            dma((4,)),
            dma((4,)),
            *([dma((2, 2))] * 8),
        ],
        compiler_params=pltpu.CompilerParams(
            collective_id=0, has_side_effects=True, vmem_limit_bytes=40 * 2**20
        ),
    )(
        *(
            pltpu.with_memory_space_constraint(x, pltpu.HBM)
            for x in (
                elevation, layover, footprint_pixel,
                footprint_device.reshape(1, tb), local_block, backscatter,
            )
        )
    )
    return pl.pallas_call(
        lookup,
        out_shape=(
            jax.ShapeDtypeStruct((held, PIX), F32),
            jax.ShapeDtypeStruct((rows, cols), F32),
        ),
        in_specs=[vmem, vmem, vmem],
        out_specs=(hbm, hbm),
        scratch_shapes=[pltpu.VMEM((rows, cols), F32), dma((1 + max(1, rows // 64),))],
        compiler_params=pltpu.CompilerParams(vmem_limit_bytes=8 * 2**20),
    )(found, places, gamma)


def solution(mesh):
    in_specs = (
        P("maprow", ("mapcol", "sect")),
        P("maprow", ("mapcol", "sect")),
        P("maprow", ("mapcol", "sect")),
        P(("maprow", "mapcol", "sect"), None, None),
        P(("maprow", "mapcol", "sect"), None),
        P(("maprow", "mapcol", "sect"), None),
    )
    out_specs = (P(("maprow", "mapcol", "sect"), None), P("maprow", ("mapcol", "sect")))
    return jax.shard_map(
        functools.partial(per_device, mesh.shape["maprow"], mesh.shape["mapcol"]),
        mesh=mesh,
        in_specs=in_specs,
        out_specs=out_specs,
        check_vma=False,
    )
```
